256 devices in a mesh: seq: 64 (over z, x, core), mp: 4 (over y).
Axes of the slice: x: 4, y: 4, z: 8, core: 2. Of those that a mesh axis runs over, the one named last changes fastest.
Arguments:
- queries: bfloat16 [65536, 1024], P('seq', 'mp'), may hold values from -8 to 8
- byte_keys: bfloat16 [65536, 1024], P('seq', 'mp'), may hold values from -8 to 8
- byte_values: bfloat16 [65536, 1024], P('seq', 'mp'), may hold values from -6 to 6
- w_query: bfloat16 [1024, 1024], P(None, 'mp'), may hold values from -0.1875 to 0.1875
- w_key: bfloat16 [1024, 1024], P(None, 'mp'), may hold values from -0.1875 to 0.1875
- w_value: bfloat16 [1024, 1024], P(None, 'mp'), may hold values from -0.1875 to 0.1875
- w_out: bfloat16 [1024, 1024], P('mp'), may hold values from -0.1875 to 0.1875
- d_output: bfloat16 [65536, 1024], P('seq'), may hold values from -96 to 96
- patch_index: int32 [65536], P('seq'), may hold values from 0 to 16383, as said below
- unpatch: bfloat16 [1024, 4096], P(None, 'mp'), may hold values from -0.09375 to 0.09375
Outputs:
- d_patch: bfloat16 [16384, 4096], P('seq', 'mp')
The draws below stay inside these ranges and needn't reach their ends.
Inputs may be any that keep to these rules, and one draw needn't show every extreme that they name: patch_index never falls and every one of the 16384 patches covers one or more bytes; patch 0 starts at byte 0, and for every k from 1 to 64 - 1 the first byte of patch k * 256 lies 1 to 128 bytes after byte k * 1024, the latter distance reached.
All inputs are finite; a program needn't handle non-finite values.
Results may differ from the reference program's by a relative error of at most 0.025.
Values may be sent and summed in bfloat16 or wider, within the bound.
No kernel may reach another device: no remote copies, remote signals or barrier semaphores. Data moves between devices by JAX's collectives and lax.ppermute only.
A program may use at most 128 MiB of HBM per device.

```python
import jax
import jax.numpy as jnp
from jax import lax

D = 1024
G = 4096
HEADS = 16
HS = 64
WINDOW = 512
BYTE_DEV = 1024
PATCH_DEV = 256
TOKENS = 65536
PATCHES = 16384


def draw_queries(key, part):
    key = jax.random.fold_in(key, 11)
    values = jax.random.normal(key, (TOKENS, HEADS * HS), jnp.float32)
    return values.astype(jnp.bfloat16)


def draw_byte_keys(key, part):
    key = jax.random.fold_in(key, 23)
    values = jax.random.normal(key, (TOKENS, HEADS * HS), jnp.float32)
    return values.astype(jnp.bfloat16)


def draw_patch_index(key, part):
    key = jax.random.fold_in(key, 5)
    owners = TOKENS // BYTE_DEV
    reach = BYTE_DEV // 8
    first_key, second_key = jax.random.split(key)
    offsets = jax.random.randint(first_key, (owners + 1,), 1, reach + 1)
    offsets = offsets.at[0].set(0).at[owners].set(0).at[1].set(reach).at[owners - 1].set(reach)
    block_starts = jnp.arange(owners + 1, dtype=jnp.int32) * BYTE_DEV + offsets
    lengths = block_starts[1:] - block_starts[:-1]
    weights = jax.random.randint(second_key, (owners, PATCH_DEV), 1, 17)
    before = jnp.cumsum(weights, axis=1) - weights
    totals = jnp.sum(weights, axis=1, keepdims=True)
    inside = before * (lengths[:, None] - PATCH_DEV) // totals + jnp.arange(PATCH_DEV, dtype=jnp.int32)[None, :]
    starts = (block_starts[:-1, None] + inside).reshape(-1)
    places = jnp.arange(TOKENS, dtype=jnp.int32)
    found = jnp.searchsorted(starts, places, side='right') - 1
    return found.astype(jnp.int32)


def block_scale(rng, dims, shards, smallest, largest):
    level, own = 1.0, jax.random.fold_in(rng, 6)
    for dim, shards_of in shards:
        heights = jnp.exp(jax.random.uniform(jax.random.fold_in(own, dim), (shards_of,), jnp.float32, smallest / len(shards), largest / len(shards)))
        level = level * jnp.repeat(heights, dims[dim] // shards_of).reshape([-1 if axis == dim else 1 for axis in range(len(dims))])
    return level


def bell_draw(rng, shape, scale, limit, cuts=(), kind=jnp.bfloat16):
    values = scale * jax.random.normal(rng, shape, jnp.float32)
    if cuts:
        values = values * block_scale(rng, shape, cuts, -0.22, 0.18)
    return jnp.clip(values, -limit, limit).astype(kind)


def setup_inputs(seed: int = 0) -> dict:
    streams_of = jax.random.split(jax.random.key(seed), 11)
    return {
        "queries": draw_queries(jax.random.fold_in(streams_of[10], 71), 0),
        "byte_keys": draw_byte_keys(jax.random.fold_in(streams_of[10], 71), 0),
        "byte_values": bell_draw(streams_of[2], (TOKENS, HEADS * HS), 1.0, 6.0, ((0, 64), (1, 4))),
        "w_query": bell_draw(streams_of[3], (D, HEADS * HS), D ** -0.5, 0.1875, ((1, 4),)),
        "w_key": bell_draw(streams_of[4], (D, HEADS * HS), D ** -0.5, 0.1875, ((1, 4),)),
        "w_value": bell_draw(streams_of[5], (D, HEADS * HS), D ** -0.5, 0.1875, ((1, 4),)),
        "w_out": bell_draw(streams_of[6], (HEADS * HS, D), (HEADS * HS) ** -0.5, 0.1875, ((0, 4),)),
        "d_output": bell_draw(streams_of[7], (TOKENS, D), 16.0, 96.0, ((0, 64),)),
        "patch_index": draw_patch_index(jax.random.fold_in(streams_of[10], 71), 0),
        "unpatch": bell_draw(streams_of[9], (D, G), G ** -0.5, 0.09375, ((1, 4),)),
    }


def block_grads(query_block, grad_block, key_block, value_block, keep_first):
    block_rows = query_block.shape[0]
    head_count = query_block.shape[1] // HS
    factor = HS ** -0.5
    query_heads = query_block.astype(jnp.float32).reshape(block_rows, head_count, HS)
    grad_heads = grad_block.astype(jnp.float32).reshape(block_rows, head_count, HS)
    key_heads = key_block.astype(jnp.float32).reshape(2 * block_rows, head_count, HS)
    value_heads = value_block.astype(jnp.float32).reshape(2 * block_rows, head_count, HS)
    scores = jnp.einsum("ihd,jhd->hij", query_heads, key_heads) * factor
    query_pos = jnp.arange(block_rows, dtype=jnp.int32)[:, None]
    key_pos = jnp.arange(2 * block_rows, dtype=jnp.int32)[None, :]
    allowed = (key_pos > query_pos) & (key_pos <= query_pos + block_rows) & ((key_pos >= block_rows) | keep_first)
    scores = jnp.where(allowed[None], scores, -1e30)
    peak = jnp.max(scores, axis=-1, keepdims=True)
    raised = jnp.exp(scores - peak)
    attend = raised / jnp.sum(raised, axis=-1, keepdims=True)
    d_attend = jnp.einsum("ihd,jhd->hij", grad_heads, value_heads)
    row_dot = jnp.sum(attend * d_attend, axis=-1, keepdims=True)
    d_scores = (attend * (d_attend - row_dot)).astype(jnp.bfloat16).astype(jnp.float32)
    attend_low = attend.astype(jnp.bfloat16).astype(jnp.float32)
    d_query = jnp.einsum("hij,jhd->ihd", d_scores, key_heads) * factor
    d_key = jnp.einsum("hij,ihd->jhd", d_scores, query_heads) * factor
    d_value = jnp.einsum("hij,ihd->jhd", attend_low, grad_heads)
    return d_query.reshape(block_rows, -1), d_key.reshape(2 * block_rows, -1), d_value.reshape(2 * block_rows, -1)


def spread(parts, width):
    leading = parts[:, :WINDOW].reshape(-1, width)
    trailing = parts[:, WINDOW:].reshape(-1, width)
    blank_rows = jnp.zeros((WINDOW, width), jnp.float32)
    return jnp.concatenate([leading, blank_rows], 0) + jnp.concatenate([blank_rows, trailing], 0)


def reference(queries, byte_keys, byte_values, w_query, w_key, w_value, w_out, d_output, patch_index, unpatch):
    width = queries.shape[1]
    grad_all = jnp.dot(d_output, w_out.T, preferred_element_type=jnp.float32).astype(jnp.bfloat16)
    blank_rows = jnp.zeros((WINDOW, width), byte_keys.dtype)
    padded_keys = jnp.concatenate([blank_rows, byte_keys], 0)
    padded_values = jnp.concatenate([blank_rows, byte_values], 0)

    def one_block(block_id):
        offset = block_id * WINDOW
        return block_grads(lax.dynamic_slice_in_dim(queries, offset, WINDOW, 0),
                           lax.dynamic_slice_in_dim(grad_all, offset, WINDOW, 0),
                           lax.dynamic_slice_in_dim(padded_keys, offset, 2 * WINDOW, 0),
                           lax.dynamic_slice_in_dim(padded_values, offset, 2 * WINDOW, 0),
                           block_id > 0)

    d_query, key_parts, value_parts = lax.map(one_block, jnp.arange(TOKENS // WINDOW, dtype=jnp.int32))
    d_query_low = d_query.reshape(TOKENS, width).astype(jnp.bfloat16)
    d_key_low = spread(key_parts, width)[WINDOW:].astype(jnp.bfloat16)
    d_value_low = spread(value_parts, width)[WINDOW:].astype(jnp.bfloat16)
    byte_grad = (jnp.dot(d_query_low, w_query.T, preferred_element_type=jnp.float32)
                 + jnp.dot(d_key_low, w_key.T, preferred_element_type=jnp.float32)
                 + jnp.dot(d_value_low, w_value.T, preferred_element_type=jnp.float32))
    patch_grad = jax.ops.segment_sum(byte_grad, patch_index, num_segments=PATCHES)
    return jnp.dot(patch_grad.astype(jnp.bfloat16), unpatch, preferred_element_type=jnp.float32).astype(jnp.bfloat16)
```

```python
import functools

import jax
import jax.numpy as jnp
from jax import lax
from jax.experimental import pallas as pl
from jax.experimental.pallas import tpu as pltpu
from jax.sharding import PartitionSpec as P

HS = 64
WINDOW = 512
PATCH_DEV = 256
TILE = 256
REACH = 128
F32 = jnp.float32
BF16 = jnp.bfloat16


def mm(a, b):
    return lax.dot_general(a, b, (((1,), (0,)), ((), ())), preferred_element_type=F32)


def mm_t(a, b):
    return lax.dot_general(a, b, (((1,), (1,)), ((), ())), preferred_element_type=F32)


def head_parts(tile):
    head = lax.broadcasted_iota(jnp.int32, tile.shape, 1) // HS
    return [jnp.where(head == h, tile, jnp.zeros_like(tile)) for h in range(tile.shape[1] // HS)]


def one_hot(slots, first, count):
    places = lax.broadcasted_iota(jnp.int32, (count, slots.shape[1]), 0) + first
    return jnp.where(places == slots, 1.0, 0.0).astype(BF16)


def attend(query, grad, keys, values, keys_t, bias):
    key_row = lax.broadcasted_iota(jnp.int32, (TILE, TILE), 0)
    query_col = lax.broadcasted_iota(jnp.int32, (TILE, TILE), 1)
    late = key_row <= query_col
    nil = jnp.zeros((TILE, TILE), BF16)
    query = query * jnp.asarray(HS**-0.5, BF16)
    d_query, d_key, d_value = [], [None] * 3, [None] * 3

    def added(total, term):
        return term if total is None else total + term

    for h, (q, g) in enumerate(zip(head_parts(query), head_parts(grad))):
        s = [mm_t(k, q) for k in keys]
        s = [x if b is None else x + b for x, b in zip(s, bias)]
        dp = [mm_t(v, g) for v in values]
        s_edge, s_mid = jnp.where(late, s[2], s[0]), s[1]
        dp_edge, dp_mid = jnp.where(late, dp[2], dp[0]), dp[1]
        peak = jnp.maximum(
            jnp.max(s_edge, axis=0, keepdims=True), jnp.max(s_mid, axis=0, keepdims=True)
        )
        e_edge, e_mid = jnp.exp(s_edge - peak), jnp.exp(s_mid - peak)
        total = jnp.sum(e_edge, axis=0, keepdims=True) + jnp.sum(e_mid, axis=0, keepdims=True)
        inverse = 1.0 / total
        row_dot = inverse * (
            jnp.sum(e_edge * dp_edge, axis=0, keepdims=True)
            + jnp.sum(e_mid * dp_mid, axis=0, keepdims=True)
        )
        p_edge, p_mid = e_edge * inverse, e_mid * inverse
        ds_edge = (p_edge * (dp_edge - row_dot)).astype(BF16)
        ds_mid = (p_mid * (dp_mid - row_dot)).astype(BF16)
        p_edge, p_mid = p_edge.astype(BF16), p_mid.astype(BF16)
        ds = [jnp.where(late, nil, ds_edge), ds_mid, jnp.where(late, ds_edge, nil)]
        p = [jnp.where(late, nil, p_edge), p_mid, jnp.where(late, p_edge, nil)]
        for t in range(3):
            d_key[t] = added(d_key[t], mm(ds[t], q))
            d_value[t] = added(d_value[t], mm(p[t], g))
        rows = slice(h * HS, (h + 1) * HS)
        d_query.append(sum(mm(keys_t[t][rows], ds[t]) for t in range(3)))
    d_query_t = jnp.concatenate(d_query, 0) * HS**-0.5
    return d_query_t.astype(BF16), d_key, d_value


def tiles_of(ref, first, count=3):
    return [ref[t * TILE : (t + 1) * TILE, :] for t in range(first, first + count)]


def near_kernel(
    d_output, w_out, queries, keys, values, slots, heads_out, k_out, v_out, x_out, kt, dk, dv, dqt
):
    later = mm_t(d_output[WINDOW:, :], w_out[...]).astype(BF16)
    for t in range(4):
        kt[t] = keys[t * TILE : (t + 1) * TILE, :].T
    for n in range(2):
        rows = slice(WINDOW + n * TILE, WINDOW + (n + 1) * TILE)
        d_query_t, d_key, d_value = attend(
            queries[rows, :],
            later[n * TILE : (n + 1) * TILE],
            tiles_of(keys, n),
            tiles_of(values, n),
            [kt[n + t] for t in range(3)],
            (None, None, None),
        )
        dqt[:, n * TILE : (n + 1) * TILE] = d_query_t
        for t in range(3):
            at = slice((n + t) * TILE, (n + t + 1) * TILE)
            if n == 0 or t == 2:
                dk[at, :] = d_key[t]
                dv[at, :] = d_value[t]
            else:
                dk[at, :] += d_key[t]
                dv[at, :] += d_value[t]
    heads_out[...] = mm_t(d_output[:WINDOW, :], w_out[...]).astype(BF16)
    k_out[...] = dk[:WINDOW, :]
    v_out[...] = dv[:WINDOW, :]
    chosen = one_hot(slots[:, WINDOW:], 0, PATCH_DEV)
    x_out[:, :TILE] = mm_t(chosen, dqt[...])
    x_out[:, TILE : 2 * TILE] = mm(chosen, dk[WINDOW:, :].astype(BF16))
    x_out[:, 2 * TILE :] = mm(chosen, dv[WINDOW:, :].astype(BF16))


def far_kernel(
    bias_ref, grads, queries, keys, values, tail_keys, tail_values, slots, tail_slots, k_in, v_in, x_in,
    sent_out, x_out, kt, dk, dv, dqt,
):
    bias = bias_ref[0]
    for t in range(2):
        kt[t] = tail_keys[t * TILE : (t + 1) * TILE, :].T
        kt[2 + t] = keys[t * TILE : (t + 1) * TILE, :].T
    all_keys = tiles_of(tail_keys, 0, 2) + tiles_of(keys, 0, 2)
    all_values = tiles_of(tail_values, 0, 2) + tiles_of(values, 0, 2)
    dk[WINDOW:, :] = k_in[...]
    dv[WINDOW:, :] = v_in[...]
    for n in range(2):
        rows = slice(n * TILE, (n + 1) * TILE)
        d_query_t, d_key, d_value = attend(
            queries[rows, :],
            grads[rows, :],
            all_keys[n : n + 3],
            all_values[n : n + 3],
            [kt[n + t] for t in range(3)],
            (bias, bias if n == 0 else None, None),
        )
        dqt[:, n * TILE : (n + 1) * TILE] = d_query_t
        for t in range(3):
            at = slice((n + t) * TILE, (n + t + 1) * TILE)
            if n == 0 and t < 2:
                dk[at, :] = d_key[t]
                dv[at, :] = d_value[t]
            else:
                dk[at, :] += d_key[t]
                dv[at, :] += d_value[t]
    before = one_hot(tail_slots[...], 0, PATCH_DEV)
    near = one_hot(slots[:, :REACH], -PATCH_DEV, PATCH_DEV)
    edge = slice(WINDOW, WINDOW + REACH)
    for place, total in ((0, dk), (PATCH_DEV, dv)):
        sent_out[place : place + PATCH_DEV, :] = (
            mm(before, total[:WINDOW, :].astype(BF16)) + mm(near, total[edge, :].astype(BF16))
        ).astype(BF16)
    sent_out[2 * PATCH_DEV :, :] = mm_t(near[PATCH_DEV - REACH :], dqt[:, :REACH]).astype(BF16)
    chosen = one_hot(slots[:, :WINDOW], 0, PATCH_DEV)
    x_out[:, :TILE] = x_in[:, :TILE] + mm_t(chosen, dqt[...])
    x_out[:, TILE : 2 * TILE] = x_in[:, TILE : 2 * TILE] + mm(chosen, dk[WINDOW:, :].astype(BF16))
    x_out[:, 2 * TILE :] = x_in[:, 2 * TILE :] + mm(chosen, dv[WINDOW:, :].astype(BF16))


def project_kernel(x_in, arrived, w_query, w_key, w_value, first_out, second_out):
    low = PATCH_DEV - REACH
    x_query = jnp.concatenate(
        [x_in[:low, :TILE], x_in[low:, :TILE] + arrived[2 * PATCH_DEV :, :].astype(F32)], 0
    ).astype(BF16)
    x_key = (x_in[:, TILE : 2 * TILE] + arrived[:PATCH_DEV, :].astype(F32)).astype(BF16)
    x_value = (
        x_in[:, 2 * TILE :] + arrived[PATCH_DEV : 2 * PATCH_DEV, :].astype(F32)
    ).astype(BF16)
    d_up = mm_t(x_query, w_query[...]) + mm_t(x_key, w_key[...]) + mm_t(x_value, w_value[...])
    first_out[...] = d_up[: PATCH_DEV // 2].astype(BF16)
    second_out[...] = d_up[PATCH_DEV // 2 :].astype(BF16)


def final_kernel(a, a_in, b, b_in, unpatch, out):
    half = PATCH_DEV // 2
    for place, own, other in ((0, a, a_in), (half, b, b_in)):
        total = (own[...].astype(F32) + other[...].astype(F32)).astype(BF16)
        out[place : place + half, :] = mm(total, unpatch[...]).astype(BF16)


def call(kernel, shapes, args, scratch=(), smem=0, flops=0):
    specs = [pl.BlockSpec(memory_space=pltpu.SMEM)] * smem
    specs += [pl.BlockSpec(memory_space=pltpu.VMEM)] * (len(args) - smem)
    return pl.pallas_call(
        kernel,
        out_shape=[jax.ShapeDtypeStruct(*shape) for shape in shapes],
        in_specs=specs,
        out_specs=[pl.BlockSpec(memory_space=pltpu.VMEM)] * len(shapes),
        scratch_shapes=list(scratch),
        compiler_params=pltpu.CompilerParams(vmem_limit_bytes=40 * 1024 * 1024),
        cost_estimate=pl.CostEstimate(flops=flops, bytes_accessed=0, transcendentals=0),
    )(*args)


def on_device(
    queries, byte_keys, byte_values, w_query, w_key, w_value, w_out, d_output, patch_index, unpatch
):
    shard = lax.axis_index("seq")
    count = lax.axis_size("seq")
    onward = [(n, n + 1) for n in range(count - 1)]
    back = [(n + 1, n) for n in range(count - 1)]
    bytes_dev = queries.shape[0]
    tail = bytes_dev - WINDOW
    tail_keys = lax.ppermute(byte_keys[tail:], "seq", onward)
    tail_values = lax.ppermute(byte_values[tail:], "seq", onward)
    slots = (patch_index - shard * PATCH_DEV)[None, :]
    tail_slots = lax.ppermute(slots[:, tail:], "seq", onward)
    bias = jnp.where(shard > 0, 0.0, -1e30).astype(F32)[None]

    grads, k_part, v_part, x_part = call(
        near_kernel,
        [((WINDOW, 256), BF16), ((WINDOW, 256), F32), ((WINDOW, 256), F32), ((PATCH_DEV, 768), F32)],
        (d_output, w_out, queries, byte_keys, byte_values, slots),
        [
            pltpu.VMEM((4, 256, TILE), BF16),
            pltpu.VMEM((1024, 256), F32),
            pltpu.VMEM((1024, 256), F32),
            pltpu.VMEM((256, 512), BF16),
        ],
        flops=8 * 10**9,
    )
    sent, x_own = call(
        far_kernel,
        [((2 * PATCH_DEV + REACH, 256), BF16), ((PATCH_DEV, 768), F32)],
        (
            bias, grads, queries, byte_keys, byte_values, tail_keys, tail_values, slots, tail_slots,
            k_part, v_part, x_part,
        ),
        [
            pltpu.VMEM((4, 256, TILE), BF16),
            pltpu.VMEM((1024, 256), F32),
            pltpu.VMEM((1024, 256), F32),
            pltpu.VMEM((256, 512), BF16),
        ],
        smem=1,
        flops=8 * 10**9,
    )
    arrived = lax.ppermute(sent, "seq", back)
    a, b = call(
        project_kernel,
        [((PATCH_DEV // 2, 1024), BF16)] * 2,
        (x_own, arrived, w_query, w_key, w_value),
        flops=4 * 10**8,
    )
    across = [(0, 1), (1, 0), (2, 3), (3, 2)]
    around = [(0, 3), (3, 0), (1, 2), (2, 1)]

    def pair(mine, other):
        return (mine.astype(F32) + other.astype(F32)).astype(BF16)

    a_in, b_in = lax.ppermute(a, "mp", across), lax.ppermute(b, "mp", around)
    a, b = pair(a, a_in), pair(b, b_in)
    a_in, b_in = lax.ppermute(a, "mp", around), lax.ppermute(b, "mp", across)
    return call(
        final_kernel,
        [((PATCH_DEV, 1024), BF16)],
        (a, a_in, b, b_in, unpatch),
        flops=5 * 10**8,
    )[0]


def solution(mesh):
    in_specs = (
        P("seq", "mp"),
        P("seq", "mp"),
        P("seq", "mp"),
        P(None, "mp"),
        P(None, "mp"),
        P(None, "mp"),
        P("mp", None),
        P("seq", None),
        P("seq"),
        P(None, "mp"),
    )
    return jax.shard_map(
        on_device, mesh=mesh, in_specs=in_specs, out_specs=P("seq", "mp"), check_vma=False
    )
```

```python
import functools

import jax
import jax.numpy as jnp
from jax import lax
from jax.experimental import pallas as pl
from jax.experimental.pallas import tpu as pltpu
from jax.sharding import PartitionSpec as P

HS = 64
WINDOW = 512
PATCH_DEV = 256
TILE = 256
REACH = 128
F32 = jnp.float32
BF16 = jnp.bfloat16


def mm(a, b):
    return lax.dot_general(a, b, (((1,), (0,)), ((), ())), preferred_element_type=F32)


def mm_t(a, b):
    return lax.dot_general(a, b, (((1,), (1,)), ((), ())), preferred_element_type=F32)


def head_parts(tile):
    head = lax.broadcasted_iota(jnp.int32, tile.shape, 1) // HS
    return [jnp.where(head == h, tile, jnp.zeros_like(tile)) for h in range(tile.shape[1] // HS)]


def one_hot(slots, first, count):
    places = lax.broadcasted_iota(jnp.int32, (count, slots.shape[1]), 0) + first
    return jnp.where(places == slots, 1.0, 0.0).astype(BF16)


def attend(query, grad, keys, values, keys_t, bias):
    key_row = lax.broadcasted_iota(jnp.int32, (TILE, TILE), 0)
    query_col = lax.broadcasted_iota(jnp.int32, (TILE, TILE), 1)
    late = key_row <= query_col
    nil = jnp.zeros((TILE, TILE), BF16)
    query = query * jnp.asarray(HS**-0.5, BF16)
    d_query, d_key, d_value = [], [None] * 3, [None] * 3

    def added(total, term):
        return term if total is None else total + term

    for h, (q, g) in enumerate(zip(head_parts(query), head_parts(grad))):
        s = [mm_t(k, q) for k in keys]
        s = [x if b is None else x + b for x, b in zip(s, bias)]
        dp = [mm_t(v, g) for v in values]
        s_edge, s_mid = jnp.where(late, s[2], s[0]), s[1]
        dp_edge, dp_mid = jnp.where(late, dp[2], dp[0]), dp[1]
        peak = jnp.maximum(
            jnp.max(s_edge, axis=0, keepdims=True), jnp.max(s_mid, axis=0, keepdims=True)
        )
        e_edge, e_mid = jnp.exp(s_edge - peak), jnp.exp(s_mid - peak)
        total = jnp.sum(e_edge, axis=0, keepdims=True) + jnp.sum(e_mid, axis=0, keepdims=True)
        inverse = 1.0 / total
        row_dot = inverse * (
            jnp.sum(e_edge * dp_edge, axis=0, keepdims=True)
            + jnp.sum(e_mid * dp_mid, axis=0, keepdims=True)
        )
        p_edge, p_mid = e_edge * inverse, e_mid * inverse
        ds_edge = (p_edge * (dp_edge - row_dot)).astype(BF16)
        ds_mid = (p_mid * (dp_mid - row_dot)).astype(BF16)
        p_edge, p_mid = p_edge.astype(BF16), p_mid.astype(BF16)
        ds = [jnp.where(late, nil, ds_edge), ds_mid, jnp.where(late, ds_edge, nil)]
        p = [jnp.where(late, nil, p_edge), p_mid, jnp.where(late, p_edge, nil)]
        for t in range(3):
            d_key[t] = added(d_key[t], mm(ds[t], q))
            d_value[t] = added(d_value[t], mm(p[t], g))
        rows = slice(h * HS, (h + 1) * HS)
        d_query.append(sum(mm(keys_t[t][rows], ds[t]) for t in range(3)))
    d_query_t = jnp.concatenate(d_query, 0) * HS**-0.5
    return d_query_t.astype(BF16), d_key, d_value


def tiles_of(ref, first, count=3):
    return [ref[t * TILE : (t + 1) * TILE, :] for t in range(first, first + count)]


def pack_kernel(shard_ref, keys, values, index, packed, sems):
    copies = [
        pltpu.make_async_copy(source.at[WINDOW:, :], packed.at[n * WINDOW : (n + 1) * WINDOW, :], sems.at[n])
        for n, source in enumerate((keys, values))
    ]
    for copy in copies:
        copy.start()
    slots = (index[:, WINDOW:] - shard_ref[0] * PATCH_DEV).astype(F32)
    row = lax.broadcasted_iota(jnp.int32, (16, TILE), 0)
    both = jnp.where(row == 0, slots[:, :TILE], slots[:, TILE:])
    packed[2 * WINDOW :, :] = both.astype(BF16)
    for copy in copies:
        copy.wait()


def heads_kernel(d_output_hbm, w_out_hbm, grads, d_output, w_out, sems):
    half = d_output.shape[0] // 2
    pairs = [(w_out_hbm, w_out)]
    pairs += [(d_output_hbm.at[n : n + half, :], d_output.at[n : n + half, :]) for n in (0, half)]
    copies = [pltpu.make_async_copy(*pair, sems.at[n]) for n, pair in enumerate(pairs)]
    for copy in copies:
        copy.start()
    copies[0].wait()
    for n in range(2):
        copies[1 + n].wait()
        rows = slice(n * half, (n + 1) * half)
        grads[rows, :] = mm_t(d_output[rows, :], w_out[...]).astype(BF16)


def place_sums(first, d_key, d_value, dk, dv, fresh=(True, True, True)):
    for t in range(3):
        at = slice((first + t) * TILE, (first + t + 1) * TILE)
        if fresh[t]:
            dk[at, :] = d_key[t]
            dv[at, :] = d_value[t]
        else:
            dk[at, :] += d_key[t]
            dv[at, :] += d_value[t]


def near_kernel(shard_ref, grads, queries, keys, values, index, near_out, x_out):
    rows = slice(2 * TILE, 3 * TILE)
    d_query_t, d_key, d_value = attend(
        queries[rows, :],
        grads[rows, :],
        tiles_of(keys, 0),
        tiles_of(values, 0),
        [keys[t * TILE : (t + 1) * TILE, :].T for t in range(3)],
        (None, None, None),
    )
    slots = index[...] - shard_ref[0] * PATCH_DEV
    d_key = jnp.concatenate([d.astype(BF16) for d in d_key], 0)
    d_value = jnp.concatenate([d.astype(BF16) for d in d_value], 0)
    before = one_hot(slots[:, :REACH], -REACH, REACH)
    near_out[:, :TILE] = mm(before, d_key[:REACH])
    near_out[:, TILE:] = mm(before, d_value[:REACH])
    chosen = one_hot(slots[:, : 3 * TILE], 0, PATCH_DEV)
    x_out[:, :TILE] = mm_t(chosen[:, 2 * TILE :], d_query_t)
    x_out[:, TILE : 2 * TILE] = mm(chosen, d_key)
    x_out[:, 2 * TILE :] = mm(chosen, d_value)


def far_kernel(
    shard_ref, grads, queries, keys, values, packed, index, near,
    sent_out, k_out, v_out, q_out, kt, dk, dv,
):
    shard = shard_ref[0]
    bias = jnp.where(shard > 0, 0.0, -1e30).astype(F32)
    slots = index[:, :REACH] - shard * PATCH_DEV
    for t in range(2):
        kt[t] = packed[t * TILE : (t + 1) * TILE, :].T
        kt[2 + t] = keys[t * TILE : (t + 1) * TILE, :].T
    all_keys = tiles_of(packed, 0, 2) + tiles_of(keys, 0, 2)
    all_values = tiles_of(packed, 2, 2) + tiles_of(values, 0, 2)
    for n in range(2):
        rows = slice(n * TILE, (n + 1) * TILE)
        d_query_t, d_key, d_value = attend(
            queries[rows, :],
            grads[rows, :],
            all_keys[n : n + 3],
            all_values[n : n + 3],
            [kt[n + t] for t in range(3)],
            (bias, bias if n == 0 else None, None),
        )
        q_out[:, rows] = d_query_t
        place_sums(n, d_key, d_value, dk, dv, (n == 0, n == 0, True))
    k_out[...] = dk[WINDOW:, :].astype(BF16)
    v_out[...] = dv[WINDOW:, :].astype(BF16)
    tail = packed[2 * WINDOW :, :].astype(F32).astype(jnp.int32)
    before = jnp.concatenate([one_hot(tail[n : n + 1], 0, PATCH_DEV) for n in range(2)], 1)
    own = one_hot(slots, -REACH, REACH)
    low = PATCH_DEV - REACH
    for n, (total, out) in enumerate(((dk, k_out), (dv, v_out))):
        place = n * PATCH_DEV
        part = mm(before, total[:WINDOW, :].astype(BF16))
        sent_out[place : place + low, :] = part[:low].astype(BF16)
        sent_out[place + low : place + PATCH_DEV, :] = (
            part[low:] + mm(own, out[:REACH, :]) + near[:, n * TILE : (n + 1) * TILE]
        ).astype(BF16)
    sent_out[2 * PATCH_DEV :, :] = mm_t(own, q_out[:, :REACH]).astype(BF16)


def last_kernel(shard_ref, grads, queries, keys, values, index, k_in, v_in, q_in, x_in, x_out):
    rows = slice(3 * TILE, 4 * TILE)
    d_query_t, d_key, d_value = attend(
        queries[rows, :],
        grads[rows, :],
        tiles_of(keys, 1),
        tiles_of(values, 1),
        [keys[t * TILE : (t + 1) * TILE, :].T for t in range(1, 4)],
        (None, None, None),
    )
    chosen = one_hot(index[...] - shard_ref[0] * PATCH_DEV, 0, PATCH_DEV)
    first, later = chosen[:, :WINDOW], chosen[:, TILE:]
    x_out[:, :TILE] = (
        x_in[:, :TILE] + mm_t(first, q_in[...]) + mm_t(chosen[:, 3 * TILE :], d_query_t)
    )
    for n, (early, parts) in enumerate(((k_in, d_key), (v_in, d_value))):
        at = slice((n + 1) * TILE, (n + 2) * TILE)
        late = jnp.concatenate([d.astype(BF16) for d in parts], 0)
        x_out[:, at] = x_in[:, at] + mm(first, early[...]) + mm(later, late)


def project_kernel(x_in, arrived, w_query, w_key, w_value, first_out, second_out):
    low = PATCH_DEV - REACH
    x_query = jnp.concatenate(
        [x_in[:low, :TILE], x_in[low:, :TILE] + arrived[2 * PATCH_DEV :, :].astype(F32)], 0
    ).astype(BF16)
    x_key = (x_in[:, TILE : 2 * TILE] + arrived[:PATCH_DEV, :].astype(F32)).astype(BF16)
    x_value = (
        x_in[:, 2 * TILE :] + arrived[PATCH_DEV : 2 * PATCH_DEV, :].astype(F32)
    ).astype(BF16)
    d_up = mm_t(x_query, w_query[...]) + mm_t(x_key, w_key[...]) + mm_t(x_value, w_value[...])
    first_out[...] = d_up[: PATCH_DEV // 2].astype(BF16)
    second_out[...] = d_up[PATCH_DEV // 2 :].astype(BF16)


def final_kernel(a, a_in, b, b_in, unpatch, out):
    half = PATCH_DEV // 2
    for place, own, other in ((0, a, a_in), (half, b, b_in)):
        total = (own[...].astype(F32) + other[...].astype(F32)).astype(BF16)
        out[place : place + half, :] = mm(total, unpatch[...]).astype(BF16)


def call(kernel, shapes, args, scratch=(), flops=0, vmem=32, whole=()):
    specs = []
    for n, arg in enumerate(args):
        space = pltpu.SMEM if arg.shape == (1,) else pl.ANY if n in whole else pltpu.VMEM
        specs.append(pl.BlockSpec(memory_space=space))
    return pl.pallas_call(
        kernel,
        out_shape=[jax.ShapeDtypeStruct(*shape) for shape in shapes],
        in_specs=specs,
        out_specs=[pl.BlockSpec(memory_space=pltpu.VMEM)] * len(shapes),
        scratch_shapes=list(scratch),
        compiler_params=pltpu.CompilerParams(vmem_limit_bytes=vmem * 1024 * 1024),
        cost_estimate=pl.CostEstimate(flops=flops, bytes_accessed=0, transcendentals=0),
    )(*args)


def on_device(
    queries, byte_keys, byte_values, w_query, w_key, w_value, w_out, d_output, patch_index, unpatch
):
    shard = lax.axis_index("seq")
    count = lax.axis_size("seq")
    onward = [(n, n + 1) for n in range(count - 1)]
    back = [(n + 1, n) for n in range(count - 1)]
    place = shard.astype(jnp.int32)[None]
    index = patch_index[None, :]
    packed = call(
        pack_kernel,
        [((2 * WINDOW + 16, 256), BF16)],
        (place, byte_keys, byte_values, index),
        [pltpu.SemaphoreType.DMA((2,))],
        flops=10**6,
        vmem=60,
        whole=(1, 2),
    )[0]
    packed = lax.ppermute(packed, "seq", onward)
    grads = call(
        heads_kernel,
        [((1024, 256), BF16)],
        (d_output, w_out),
        [pltpu.VMEM((1024, 1024), BF16), pltpu.VMEM((256, 1024), BF16), pltpu.SemaphoreType.DMA((3,))],
        flops=8 * 10**9,
        vmem=58,
        whole=(0, 1),
    )[0]
    own = (place, grads, queries, byte_keys, byte_values)
    near, x_near = call(
        near_kernel,
        [((REACH, 512), F32), ((PATCH_DEV, 768), F32)],
        (*own, index),
        flops=8 * 10**9,
    )
    sent, k_part, v_part, q_part = call(
        far_kernel,
        [((2 * PATCH_DEV + REACH, 256), BF16), ((WINDOW, 256), BF16), ((WINDOW, 256), BF16), ((256, WINDOW), BF16)],
        (*own, packed, index, near),
        [pltpu.VMEM((4, 256, TILE), BF16), pltpu.VMEM((1024, 256), F32), pltpu.VMEM((1024, 256), F32)],
        flops=8 * 10**9,
    )
    arrived = lax.ppermute(sent, "seq", back)
    x_own = call(
        last_kernel,
        [((PATCH_DEV, 768), F32)],
        (*own, index, k_part, v_part, q_part, x_near),
        flops=8 * 10**9,
    )[0]
    a, b = call(
        project_kernel,
        [((PATCH_DEV // 2, 1024), BF16)] * 2,
        (x_own, arrived, w_query, w_key, w_value),
        flops=4 * 10**8,
    )
    across = [(0, 1), (1, 0), (2, 3), (3, 2)]
    around = [(0, 3), (3, 0), (1, 2), (2, 1)]

    def pair(mine, other):
        return (mine.astype(F32) + other.astype(F32)).astype(BF16)

    a_in, b_in = lax.ppermute(a, "mp", across), lax.ppermute(b, "mp", around)
    a, b = pair(a, a_in), pair(b, b_in)
    a_in, b_in = lax.ppermute(a, "mp", around), lax.ppermute(b, "mp", across)
    return call(
        final_kernel,
        [((PATCH_DEV, 1024), BF16)],
        (a, a_in, b, b_in, unpatch),
        flops=5 * 10**8,
    )[0]


def solution(mesh):
    in_specs = (
        P("seq", "mp"),
        P("seq", "mp"),
        P("seq", "mp"),
        P(None, "mp"),
        P(None, "mp"),
        P(None, "mp"),
        P("mp", None),
        P("seq", None),
        P("seq"),
        P(None, "mp"),
    )
    return jax.shard_map(
        on_device, mesh=mesh, in_specs=in_specs, out_specs=P("seq", "mp"), check_vma=False
    )
```

```python
import functools

import jax
import jax.numpy as jnp
from jax import lax
from jax.experimental import pallas as pl
from jax.experimental.pallas import tpu as pltpu
from jax.sharding import PartitionSpec as P

HS = 64
WINDOW = 512
PATCH_DEV = 256
TILE = 256
REACH = 128
STRIP = 32
F32 = jnp.float32
BF16 = jnp.bfloat16


def mm(a, b):
    return lax.dot_general(a, b, (((1,), (0,)), ((), ())), preferred_element_type=F32)


def mm_t(a, b):
    return lax.dot_general(a, b, (((1,), (1,)), ((), ())), preferred_element_type=F32)


def head_parts(tile):
    head = lax.broadcasted_iota(jnp.int32, tile.shape, 1) // HS
    return [jnp.where(head == h, tile, jnp.zeros_like(tile)) for h in range(tile.shape[1] // HS)]


def one_hot(slots, first, count):
    places = lax.broadcasted_iota(jnp.int32, (count, slots.shape[1]), 0) + first
    return jnp.where(places == slots, 1.0, 0.0).astype(BF16)


def rows_of_8(x, reduce):
    return reduce(x.reshape(x.shape[0] // 8, 8, x.shape[1]), 0)


def joined(total, term, op=jnp.add):
    return term if total is None else op(total, term)


class Unit:
    def __init__(self, keys, values, keys_t, query, grad, far_bias, mid_bias):
        self.keys, self.values, self.keys_t = keys, values, keys_t
        self.query, self.grad = query, grad
        self.far_bias, self.mid_bias = far_bias, mid_bias
        self.s, self.dp = [None] * 3, [None] * 3
        self.d_key, self.d_value = [None] * 3, [None] * 3
        self.strips, self.low = {}, {}
        self.peak = self.total = self.dot = None

    def score_steps(self):
        def step(into, t, a, b):
            into[t] = mm_t(a, b)

        steps = [functools.partial(step, self.s, t, self.keys[t], self.query) for t in (0, 2, 1)]
        return steps + [functools.partial(step, self.dp, t, self.values[t], self.grad) for t in (0, 2, 1)]

    def back_steps(self):
        def step(into, t, a, b):
            into[t] = mm(a[t], b)

        def query_step():
            self.d_query_t = mm(self.keys_t, jnp.concatenate(self.ds, 0))

        steps = []
        for t in range(3):
            steps.append(functools.partial(step, self.d_key, t, self.ds, self.query))
            steps.append(functools.partial(step, self.d_value, t, self.p, self.grad))
        return steps[:3] + [query_step] + steps[3:]

    def inside(self, row):
        shape = (STRIP, TILE // 2)
        ahead = lax.broadcasted_iota(jnp.int32, shape, 1) - lax.broadcasted_iota(jnp.int32, shape, 0)
        return ahead >= row % (TILE // 2)

    def edge(self, parts, row, bias=None):
        half = TILE // 2
        far, near = parts[0][row : row + STRIP], parts[2][row : row + STRIP]
        if bias is not None:
            far = far + bias
        if row < half:
            left, right = jnp.where(self.inside(row), near[:, :half], far[:, :half]), near[:, half:]
        else:
            left, right = far[:, :half], jnp.where(self.inside(row), near[:, half:], far[:, half:])
        return jnp.concatenate([left, right], 1)

    def parted(self, x, row):
        half = TILE // 2
        left, right = x[:, :half], x[:, half:]
        nil = jnp.zeros_like(left)
        ok = self.inside(row)
        if row < half:
            near, far = [jnp.where(ok, left, nil), right], [jnp.where(ok, nil, left), nil]
        else:
            near, far = [nil, jnp.where(ok, right, nil)], [left, jnp.where(ok, nil, right)]
        return jnp.concatenate(far, 1), jnp.concatenate(near, 1)

    def strip_of(self, parts, mid, row):
        return parts[1][row : row + STRIP] if mid else self.edge(parts, row)

    def soft_steps(self):
        places = [(mid, row) for mid in (False, True) for row in range(0, TILE, STRIP)]

        def peak_step(mid, row):
            if mid:
                x = self.s[1][row : row + STRIP]
                x = x if self.mid_bias is None else x + self.mid_bias
            else:
                x = self.edge(self.s, row, self.far_bias)
            self.strips[mid, row] = x
            self.peak = joined(self.peak, rows_of_8(x, jnp.max), jnp.maximum)

        def peak_end():
            self.peak = jnp.max(self.peak, axis=0, keepdims=True)

        def exp_step(mid, row):
            e = jnp.exp(self.strips[mid, row] - self.peak)
            self.strips[mid, row] = e
            self.total = joined(self.total, rows_of_8(e, jnp.sum))
            self.dot = joined(self.dot, rows_of_8(e * self.strip_of(self.dp, mid, row), jnp.sum))

        def exp_end():
            self.inverse = 1.0 / jnp.sum(self.total, axis=0, keepdims=True)
            self.row_dot = self.inverse * jnp.sum(self.dot, axis=0, keepdims=True)

        def low_step(mid, row):
            p = self.strips[mid, row] * self.inverse
            ds = p * (self.strip_of(self.dp, mid, row) - self.row_dot)
            for name, x in (("p", p), ("ds", ds)):
                if mid:
                    self.low[name, 1, row] = x.astype(BF16)
                else:
                    far, near = self.parted(x, row)
                    self.low[name, 0, row], self.low[name, 2, row] = far.astype(BF16), near.astype(BF16)

        def low_end():
            self.p, self.ds = (
                [
                    jnp.concatenate([self.low[name, t, row] for row in range(0, TILE, STRIP)], 0)
                    for t in range(3)
                ]
                for name in ("p", "ds")
            )

        steps = []
        for step, end in ((peak_step, peak_end), (exp_step, exp_end), (low_step, low_end)):
            steps += [functools.partial(step, *place) for place in places] + [end]
        return steps


def attend(tiles):
    units = []
    for query, grad, keys, values, far_bias, mid_bias in tiles:
        keys_t = jnp.concatenate([k.T for k in keys], 1)
        q_heads = head_parts(query * jnp.asarray(HS**-0.5, BF16))
        for h, (q, g) in enumerate(zip(q_heads, head_parts(grad))):
            units.append(Unit(keys, values, keys_t[h * HS : (h + 1) * HS], q, g, far_bias, mid_bias))
    for n in range(len(units) + 2):
        matmuls = units[n - 2].back_steps() if n >= 2 else []
        matmuls += units[n].score_steps() if n < len(units) else []
        strips = units[n - 1].soft_steps() if 1 <= n <= len(units) else []
        done = 0
        for place, step in enumerate(strips):
            step()
            while done < (place + 1) * len(matmuls) // len(strips):
                matmuls[done]()
                done += 1
        for step in matmuls[done:]:
            step()
    out = []
    heads = len(units) // len(tiles)
    for first in range(0, len(units), heads):
        own = units[first : first + heads]
        d_query_t = jnp.concatenate([unit.d_query_t for unit in own], 0) * HS**-0.5
        d_key = [sum(unit.d_key[t] for unit in own) for t in range(3)]
        d_value = [sum(unit.d_value[t] for unit in own) for t in range(3)]
        out.append((d_query_t.astype(BF16), d_key, d_value))
    return out


def tiles_of(ref, first, count=3):
    return [ref[t * TILE : (t + 1) * TILE, :] for t in range(first, first + count)]


def whole_low(parts):
    return jnp.concatenate([part.astype(BF16) for part in parts], 0)


def pack_kernel(shard_ref, keys, values, index, packed, sems):
    copies = [
        pltpu.make_async_copy(source.at[WINDOW:, :], packed.at[n * WINDOW : (n + 1) * WINDOW, :], sems.at[n])
        for n, source in enumerate((keys, values))
    ]
    for copy in copies:
        copy.start()
    slots = (index[:, WINDOW:] - shard_ref[0] * PATCH_DEV).astype(F32)
    row = lax.broadcasted_iota(jnp.int32, (16, TILE), 0)
    both = jnp.where(row == 0, slots[:, :TILE], slots[:, TILE:])
    packed[2 * WINDOW :, :] = both.astype(BF16)
    for copy in copies:
        copy.wait()


def heads_kernel(d_output_hbm, w_out_hbm, grads, d_output, w_out, sems):
    half = d_output.shape[0] // 2
    pairs = [(w_out_hbm, w_out)]
    pairs += [(d_output_hbm.at[n : n + half, :], d_output.at[n : n + half, :]) for n in (0, half)]
    copies = [pltpu.make_async_copy(*pair, sems.at[n]) for n, pair in enumerate(pairs)]
    for copy in copies:
        copy.start()
    copies[0].wait()
    for n in range(2):
        copies[1 + n].wait()
        rows = slice(n * half, (n + 1) * half)
        grads[rows, :] = mm_t(d_output[rows, :], w_out[...]).astype(BF16)


def near_kernel(shard_ref, grads, queries, keys, values, index, near_out, x_out):
    rows = slice(2 * TILE, 3 * TILE)
    d_query_t, d_key, d_value = attend(
        [(queries[rows, :], grads[rows, :], tiles_of(keys, 0), tiles_of(values, 0), None, None)]
    )[0]
    slots = index[...] - shard_ref[0] * PATCH_DEV
    d_key, d_value = whole_low(d_key), whole_low(d_value)
    before = one_hot(slots[:, :REACH], -REACH, REACH)
    near_out[:, :TILE] = mm(before, d_key[:REACH])
    near_out[:, TILE:] = mm(before, d_value[:REACH])
    chosen = one_hot(slots[:, : 3 * TILE], 0, PATCH_DEV)
    x_out[:, :TILE] = mm_t(chosen[:, 2 * TILE :], d_query_t)
    x_out[:, TILE : 2 * TILE] = mm(chosen, d_key)
    x_out[:, 2 * TILE :] = mm(chosen, d_value)


def far_kernel(
    shard_ref, grads, queries, keys, values, packed, index, near,
    sent_out, k_out, v_out, q_out,
):
    shard = shard_ref[0]
    bias = jnp.where(shard > 0, 0.0, -1e30).astype(F32)
    slots = index[:, :REACH] - shard * PATCH_DEV
    all_keys = tiles_of(packed, 0, 2) + tiles_of(keys, 0, 2)
    all_values = tiles_of(packed, 2, 2) + tiles_of(values, 0, 2)
    tiles = []
    for n in range(2):
        rows = slice(n * TILE, (n + 1) * TILE)
        tiles.append(
            (queries[rows, :], grads[rows, :], all_keys[n : n + 3], all_values[n : n + 3], bias, None if n else bias)
        )
    (q_first, *first), (q_second, *second) = attend(tiles)
    q_out[:, :TILE], q_out[:, TILE:] = q_first, q_second
    tail = packed[2 * WINDOW :, :].astype(F32).astype(jnp.int32)
    before = jnp.concatenate([one_hot(tail[n : n + 1], 0, PATCH_DEV) for n in range(2)], 1)
    own = one_hot(slots, -REACH, REACH)
    low = PATCH_DEV - REACH
    for n, (a, b, out) in enumerate(zip(first, second, (k_out, v_out))):
        place = n * PATCH_DEV
        gone = whole_low([a[0], a[1] + b[0]])
        out[...] = whole_low([a[2] + b[1], b[2]])
        part = mm(before, gone)
        sent_out[place : place + low, :] = part[:low].astype(BF16)
        sent_out[place + low : place + PATCH_DEV, :] = (
            part[low:] + mm(own, out[:REACH, :]) + near[:, n * TILE : (n + 1) * TILE]
        ).astype(BF16)
    sent_out[2 * PATCH_DEV :, :] = mm_t(own, q_out[:, :REACH]).astype(BF16)


def last_kernel(shard_ref, grads, queries, keys, values, index, k_in, v_in, q_in, x_in, x_out):
    rows = slice(3 * TILE, 4 * TILE)
    d_query_t, d_key, d_value = attend(
        [(queries[rows, :], grads[rows, :], tiles_of(keys, 1), tiles_of(values, 1), None, None)]
    )[0]
    chosen = one_hot(index[...] - shard_ref[0] * PATCH_DEV, 0, PATCH_DEV)
    first, later = chosen[:, :WINDOW], chosen[:, TILE:]
    x_out[:, :TILE] = (
        x_in[:, :TILE] + mm_t(first, q_in[...]) + mm_t(chosen[:, 3 * TILE :], d_query_t)
    )
    for n, (early, parts) in enumerate(((k_in, d_key), (v_in, d_value))):
        at = slice((n + 1) * TILE, (n + 2) * TILE)
        x_out[:, at] = x_in[:, at] + mm(first, early[...]) + mm(later, whole_low(parts))


def project_kernel(x_in, arrived, w_query, w_key, w_value, first_out, second_out):
    low = PATCH_DEV - REACH
    x_query = jnp.concatenate(
        [x_in[:low, :TILE], x_in[low:, :TILE] + arrived[2 * PATCH_DEV :, :].astype(F32)], 0
    ).astype(BF16)
    x_key = (x_in[:, TILE : 2 * TILE] + arrived[:PATCH_DEV, :].astype(F32)).astype(BF16)
    x_value = (
        x_in[:, 2 * TILE :] + arrived[PATCH_DEV : 2 * PATCH_DEV, :].astype(F32)
    ).astype(BF16)
    d_up = mm_t(x_query, w_query[...]) + mm_t(x_key, w_key[...]) + mm_t(x_value, w_value[...])
    first_out[...] = d_up[: PATCH_DEV // 2].astype(BF16)
    second_out[...] = d_up[PATCH_DEV // 2 :].astype(BF16)


def final_kernel(a, a_in, b, b_in, unpatch, out):
    half = PATCH_DEV // 2
    for place, own, other in ((0, a, a_in), (half, b, b_in)):
        total = (own[...].astype(F32) + other[...].astype(F32)).astype(BF16)
        out[place : place + half, :] = mm(total, unpatch[...]).astype(BF16)


def call(kernel, shapes, args, scratch=(), flops=0, vmem=32, whole=()):
    specs = []
    for n, arg in enumerate(args):
        space = pltpu.SMEM if arg.shape == (1,) else pl.ANY if n in whole else pltpu.VMEM
        specs.append(pl.BlockSpec(memory_space=space))
    return pl.pallas_call(
        kernel,
        out_shape=[jax.ShapeDtypeStruct(*shape) for shape in shapes],
        in_specs=specs,
        out_specs=[pl.BlockSpec(memory_space=pltpu.VMEM)] * len(shapes),
        scratch_shapes=list(scratch),
        compiler_params=pltpu.CompilerParams(vmem_limit_bytes=vmem * 1024 * 1024),
        cost_estimate=pl.CostEstimate(flops=flops, bytes_accessed=0, transcendentals=0),
    )(*args)


def on_device(
    queries, byte_keys, byte_values, w_query, w_key, w_value, w_out, d_output, patch_index, unpatch
):
    shard = lax.axis_index("seq")
    count = lax.axis_size("seq")
    onward = [(n, n + 1) for n in range(count - 1)]
    back = [(n + 1, n) for n in range(count - 1)]
    place = shard.astype(jnp.int32)[None]
    index = patch_index[None, :]
    packed = call(
        pack_kernel,
        [((2 * WINDOW + 16, 256), BF16)],
        (place, byte_keys, byte_values, index),
        [pltpu.SemaphoreType.DMA((2,))],
        flops=10**6,
        vmem=60,
        whole=(1, 2),
    )[0]
    packed = lax.ppermute(packed, "seq", onward)
    grads = call(
        heads_kernel,
        [((1024, 256), BF16)],
        (d_output, w_out),
        [pltpu.VMEM((1024, 1024), BF16), pltpu.VMEM((256, 1024), BF16), pltpu.SemaphoreType.DMA((3,))],
        flops=8 * 10**9,
        vmem=58,
        whole=(0, 1),
    )[0]
    own = (place, grads, queries, byte_keys, byte_values)
    near, x_near = call(
        near_kernel,
        [((REACH, 512), F32), ((PATCH_DEV, 768), F32)],
        (*own, index),
        flops=8 * 10**9,
    )
    sent, k_part, v_part, q_part = call(
        far_kernel,
        [((2 * PATCH_DEV + REACH, 256), BF16), ((WINDOW, 256), BF16), ((WINDOW, 256), BF16), ((256, WINDOW), BF16)],
        (*own, packed, index, near),
        flops=8 * 10**9,
    )
    arrived = lax.ppermute(sent, "seq", back)
    x_own = call(
        last_kernel,
        [((PATCH_DEV, 768), F32)],
        (*own, index, k_part, v_part, q_part, x_near),
        flops=8 * 10**9,
    )[0]
    a, b = call(
        project_kernel,
        [((PATCH_DEV // 2, 1024), BF16)] * 2,
        (x_own, arrived, w_query, w_key, w_value),
        flops=4 * 10**8,
    )
    across = [(0, 1), (1, 0), (2, 3), (3, 2)]
    around = [(0, 3), (3, 0), (1, 2), (2, 1)]

    def pair(mine, other):
        return (mine.astype(F32) + other.astype(F32)).astype(BF16)

    a_in, b_in = lax.ppermute(a, "mp", across), lax.ppermute(b, "mp", around)
    a, b = pair(a, a_in), pair(b, b_in)
    a_in, b_in = lax.ppermute(a, "mp", around), lax.ppermute(b, "mp", across)
    return call(
        final_kernel,
        [((PATCH_DEV, 1024), BF16)],
        (a, a_in, b, b_in, unpatch),
        flops=5 * 10**8,
    )[0]


def solution(mesh):
    in_specs = (
        P("seq", "mp"),
        P("seq", "mp"),
        P("seq", "mp"),
        P(None, "mp"),
        P(None, "mp"),
        P(None, "mp"),
        P("mp", None),
        P("seq", None),
        P("seq"),
        P(None, "mp"),
    )
    return jax.shard_map(
        on_device, mesh=mesh, in_specs=in_specs, out_specs=P("seq", "mp"), check_vma=False
    )
```

```python
import functools

import jax
import jax.numpy as jnp
from jax import lax
from jax.experimental import pallas as pl
from jax.experimental.pallas import tpu as pltpu
from jax.sharding import PartitionSpec as P

HS = 64
WINDOW = 512
PATCH_DEV = 256
TILE = 256
REACH = 128
STRIP = 32
F32 = jnp.float32
BF16 = jnp.bfloat16


def mm(a, b):
    return lax.dot_general(a, b, (((1,), (0,)), ((), ())), preferred_element_type=F32)


def mm_t(a, b):
    return lax.dot_general(a, b, (((1,), (1,)), ((), ())), preferred_element_type=F32)


def head_parts(tile):
    head = lax.broadcasted_iota(jnp.int32, tile.shape, 1) // HS
    return [jnp.where(head == h, tile, jnp.zeros_like(tile)) for h in range(tile.shape[1] // HS)]


def one_hot(slots, first, count):
    places = lax.broadcasted_iota(jnp.int32, (count, slots.shape[1]), 0) + first
    return jnp.where(places == slots, 1.0, 0.0).astype(BF16)


def rows_of_8(x, reduce):
    return reduce(x.reshape(x.shape[0] // 8, 8, x.shape[1]), 0)


def joined(total, term, op=jnp.add):
    return term if total is None else op(total, term)


class Unit:
    def __init__(self, keys, values, keys_t, query, grad, far_bias, mid_bias):
        self.keys, self.values, self.keys_t = keys, values, keys_t
        self.query, self.grad = query, grad
        self.far_bias, self.mid_bias = far_bias, mid_bias
        self.s, self.dp = [None] * 3, [None] * 3
        self.d_key, self.d_value = [None] * 3, [None] * 3
        self.strips, self.low = {}, {}
        self.peak = self.total = self.dot = None

    def score_steps(self):
        def step(into, t, a, b):
            into[t] = mm_t(a, b)

        steps = [functools.partial(step, self.s, t, self.keys[t], self.query) for t in (0, 2, 1)]
        return steps + [functools.partial(step, self.dp, t, self.values[t], self.grad) for t in (0, 2, 1)]

    def back_steps(self):
        def step(into, t, a, b):
            into[t] = mm(a[t], b)

        def query_step():
            self.d_query_t = mm(self.keys_t, jnp.concatenate(self.ds, 0))

        steps = []
        for t in range(3):
            steps.append(functools.partial(step, self.d_key, t, self.ds, self.query))
            steps.append(functools.partial(step, self.d_value, t, self.p, self.grad))
        return steps[:3] + [query_step] + steps[3:]

    def inside(self, row):
        shape = (STRIP, TILE // 2)
        ahead = lax.broadcasted_iota(jnp.int32, shape, 1) - lax.broadcasted_iota(jnp.int32, shape, 0)
        return ahead >= row % (TILE // 2)

    def edge(self, parts, row, bias=None):
        half = TILE // 2
        far, near = parts[0][row : row + STRIP], parts[2][row : row + STRIP]
        if bias is not None:
            far = far + bias
        if row < half:
            left, right = jnp.where(self.inside(row), near[:, :half], far[:, :half]), near[:, half:]
        else:
            left, right = far[:, :half], jnp.where(self.inside(row), near[:, half:], far[:, half:])
        return jnp.concatenate([left, right], 1)

    def parted(self, x, row):
        half = TILE // 2
        left, right = x[:, :half], x[:, half:]
        nil = jnp.zeros_like(left)
        ok = self.inside(row)
        if row < half:
            near, far = [jnp.where(ok, left, nil), right], [jnp.where(ok, nil, left), nil]
        else:
            near, far = [nil, jnp.where(ok, right, nil)], [left, jnp.where(ok, nil, right)]
        return jnp.concatenate(far, 1), jnp.concatenate(near, 1)

    def strip_of(self, parts, mid, row):
        return parts[1][row : row + STRIP] if mid else self.edge(parts, row)

    def soft_steps(self):
        places = [(mid, row) for mid in (False, True) for row in range(0, TILE, STRIP)]

        def peak_step(mid, row):
            if mid:
                x = self.s[1][row : row + STRIP]
                x = x if self.mid_bias is None else x + self.mid_bias
            else:
                x = self.edge(self.s, row, self.far_bias)
            self.strips[mid, row] = x
            self.peak = joined(self.peak, rows_of_8(x, jnp.max), jnp.maximum)

        def peak_end():
            self.peak = jnp.max(self.peak, axis=0, keepdims=True)

        def exp_step(mid, row):
            e = jnp.exp(self.strips[mid, row] - self.peak)
            self.strips[mid, row] = e
            self.total = joined(self.total, rows_of_8(e, jnp.sum))
            self.dot = joined(self.dot, rows_of_8(e * self.strip_of(self.dp, mid, row), jnp.sum))

        def exp_end():
            self.inverse = 1.0 / jnp.sum(self.total, axis=0, keepdims=True)
            self.row_dot = self.inverse * jnp.sum(self.dot, axis=0, keepdims=True)

        def low_step(mid, row):
            p = self.strips[mid, row] * self.inverse
            ds = p * (self.strip_of(self.dp, mid, row) - self.row_dot)
            for name, x in (("p", p), ("ds", ds)):
                if mid:
                    self.low[name, 1, row] = x.astype(BF16)
                else:
                    far, near = self.parted(x, row)
                    self.low[name, 0, row], self.low[name, 2, row] = far.astype(BF16), near.astype(BF16)

        def low_end():
            self.p, self.ds = (
                [
                    jnp.concatenate([self.low[name, t, row] for row in range(0, TILE, STRIP)], 0)
                    for t in range(3)
                ]
                for name in ("p", "ds")
            )

        steps = []
        for step, end in ((peak_step, peak_end), (exp_step, exp_end), (low_step, low_end)):
            steps += [functools.partial(step, *place) for place in places] + [end]
        return steps


def attend(tiles):
    units = []
    for query, grad, keys, values, far_bias, mid_bias in tiles:
        keys_t = jnp.concatenate([k.T for k in keys], 1)
        q_heads = head_parts(query * jnp.asarray(HS**-0.5, BF16))
        for h, (q, g) in enumerate(zip(q_heads, head_parts(grad))):
            units.append(Unit(keys, values, keys_t[h * HS : (h + 1) * HS], q, g, far_bias, mid_bias))
    for n in range(len(units) + 2):
        matmuls = units[n - 2].back_steps() if n >= 2 else []
        matmuls += units[n].score_steps() if n < len(units) else []
        strips = units[n - 1].soft_steps() if 1 <= n <= len(units) else []
        done = 0
        for place, step in enumerate(strips):
            step()
            while done < (place + 1) * len(matmuls) // len(strips):
                matmuls[done]()
                done += 1
        for step in matmuls[done:]:
            step()
    out = []
    heads = len(units) // len(tiles)
    for first in range(0, len(units), heads):
        own = units[first : first + heads]
        d_query_t = jnp.concatenate([unit.d_query_t for unit in own], 0) * HS**-0.5
        d_key = [sum(unit.d_key[t] for unit in own) for t in range(3)]
        d_value = [sum(unit.d_value[t] for unit in own) for t in range(3)]
        out.append((d_query_t.astype(BF16), d_key, d_value))
    return out


def tiles_of(ref, first, count=3):
    return [ref[t * TILE : (t + 1) * TILE, :] for t in range(first, first + count)]


def whole_low(parts):
    return jnp.concatenate([part.astype(BF16) for part in parts], 0)


def pack_kernel(keys, values, index_hbm, packed, index, held, sems, out_sems):
    arriving, leaving = [], []
    for n in range(4):
        source = (keys, values)[n // 2]
        first = WINDOW + n % 2 * TILE
        rows = slice(n * TILE, (n + 1) * TILE)
        arriving.append(pltpu.make_async_copy(source.at[first : first + TILE, :], held.at[rows, :], sems.at[n]))
        leaving.append(pltpu.make_async_copy(held.at[rows, :], packed.at[rows, :], out_sems.at[n]))
    places = pltpu.make_async_copy(index_hbm, index, sems.at[4])
    for copy in (places, *arriving):
        copy.start()
    places.wait()
    slots = (index[:, WINDOW:] & (PATCH_DEV - 1)).astype(F32)
    row = lax.broadcasted_iota(jnp.int32, (16, TILE), 0)
    both = jnp.where(row == 0, slots[:, :TILE], slots[:, TILE:])
    held[2 * WINDOW :, :] = both.astype(BF16)
    slots_leaving = pltpu.make_async_copy(
        held.at[2 * WINDOW :, :], packed.at[2 * WINDOW :, :], out_sems.at[4]
    )
    slots_leaving.start()
    for copy, onward in zip(arriving, leaving):
        copy.wait()
        onward.start()
    for onward in leaving:
        onward.wait()
    slots_leaving.wait()


def heads_kernel(d_output_hbm, w_out_hbm, grads, d_output, w_out, sems):
    half = d_output.shape[0] // 2
    pairs = [(w_out_hbm, w_out)]
    pairs += [(d_output_hbm.at[n : n + half, :], d_output.at[n : n + half, :]) for n in (0, half)]
    copies = [pltpu.make_async_copy(*pair, sems.at[n]) for n, pair in enumerate(pairs)]
    for copy in copies:
        copy.start()
    copies[0].wait()
    for n in range(2):
        copies[1 + n].wait()
        rows = slice(n * half, (n + 1) * half)
        grads[rows, :] = mm_t(d_output[rows, :], w_out[...]).astype(BF16)


def near_kernel(grads, queries, keys, values, index, near_out, x_out):
    rows = slice(2 * TILE, 3 * TILE)
    d_query_t, d_key, d_value = attend(
        [(queries[rows, :], grads[rows, :], tiles_of(keys, 0), tiles_of(values, 0), None, None)]
    )[0]
    slots = index[...] - lax.axis_index("seq") * PATCH_DEV
    d_key, d_value = whole_low(d_key), whole_low(d_value)
    before = one_hot(slots[:, :REACH], -REACH, REACH)
    near_out[:, :TILE] = mm(before, d_key[:REACH])
    near_out[:, TILE:] = mm(before, d_value[:REACH])
    chosen = one_hot(slots[:, : 3 * TILE], 0, PATCH_DEV)
    x_out[:, :TILE] = mm_t(chosen[:, 2 * TILE :], d_query_t)
    x_out[:, TILE : 2 * TILE] = mm(chosen, d_key)
    x_out[:, 2 * TILE :] = mm(chosen, d_value)


def far_kernel(
    grads, queries, keys, values, packed, index, near,
    sent_out, k_out, v_out, q_out,
):
    shard = lax.axis_index("seq")
    bias = jnp.where(shard > 0, 0.0, -1e30).astype(F32)
    slots = index[:, :REACH] - shard * PATCH_DEV
    all_keys = tiles_of(packed, 0, 2) + tiles_of(keys, 0, 2)
    all_values = tiles_of(packed, 2, 2) + tiles_of(values, 0, 2)
    tiles = []
    for n in range(2):
        rows = slice(n * TILE, (n + 1) * TILE)
        tiles.append(
            (queries[rows, :], grads[rows, :], all_keys[n : n + 3], all_values[n : n + 3], bias, None if n else bias)
        )
    (q_first, *first), (q_second, *second) = attend(tiles)
    q_out[:, :TILE], q_out[:, TILE:] = q_first, q_second
    tail = packed[2 * WINDOW :, :].astype(F32).astype(jnp.int32)
    before = jnp.concatenate([one_hot(tail[n : n + 1], 0, PATCH_DEV) for n in range(2)], 1)
    own = one_hot(slots, -REACH, REACH)
    low = PATCH_DEV - REACH
    for n, (a, b, out) in enumerate(zip(first, second, (k_out, v_out))):
        place = n * PATCH_DEV
        gone = whole_low([a[0], a[1] + b[0]])
        out[...] = whole_low([a[2] + b[1], b[2]])
        part = mm(before, gone)
        sent_out[place : place + low, :] = part[:low].astype(BF16)
        sent_out[place + low : place + PATCH_DEV, :] = (
            part[low:] + mm(own, out[:REACH, :]) + near[:, n * TILE : (n + 1) * TILE]
        ).astype(BF16)
    sent_out[2 * PATCH_DEV :, :] = mm_t(own, q_out[:, :REACH]).astype(BF16)


def last_kernel(grads, queries, keys, values, index, k_in, v_in, q_in, x_in, x_out):
    rows = slice(3 * TILE, 4 * TILE)
    d_query_t, d_key, d_value = attend(
        [(queries[rows, :], grads[rows, :], tiles_of(keys, 1), tiles_of(values, 1), None, None)]
    )[0]
    chosen = one_hot(index[...] - lax.axis_index("seq") * PATCH_DEV, 0, PATCH_DEV)
    first, later = chosen[:, :WINDOW], chosen[:, TILE:]
    x_out[:, :TILE] = (
        x_in[:, :TILE] + mm_t(first, q_in[...]) + mm_t(chosen[:, 3 * TILE :], d_query_t)
    )
    for n, (early, parts) in enumerate(((k_in, d_key), (v_in, d_value))):
        at = slice((n + 1) * TILE, (n + 2) * TILE)
        x_out[:, at] = x_in[:, at] + mm(first, early[...]) + mm(later, whole_low(parts))


def project_kernel(x_in, arrived, w_query, w_key, w_value, first_out, second_out):
    low = PATCH_DEV - REACH
    x_query = jnp.concatenate(
        [x_in[:low, :TILE], x_in[low:, :TILE] + arrived[2 * PATCH_DEV :, :].astype(F32)], 0
    ).astype(BF16)
    x_key = (x_in[:, TILE : 2 * TILE] + arrived[:PATCH_DEV, :].astype(F32)).astype(BF16)
    x_value = (
        x_in[:, 2 * TILE :] + arrived[PATCH_DEV : 2 * PATCH_DEV, :].astype(F32)
    ).astype(BF16)
    d_up = mm_t(x_query, w_query[...]) + mm_t(x_key, w_key[...]) + mm_t(x_value, w_value[...])
    first_out[...] = d_up[: PATCH_DEV // 2].astype(BF16)
    second_out[...] = d_up[PATCH_DEV // 2 :].astype(BF16)


def final_kernel(first, mine, other, unpatch, *refs):
    out, low, sems = refs[-3:]
    total = (mine[...].astype(F32) + other[...].astype(F32)).astype(BF16)
    half = PATCH_DEV // 2
    width = low.shape[1] // sems.shape[0]
    copies = []
    for n in range(sems.shape[0]):
        at = slice(n * width, (n + 1) * width)
        low[:, at] = mm(total, unpatch[:, at]).astype(BF16)
        copies.append(pltpu.make_async_copy(low.at[:, at], out.at[first : first + half, at], sems.at[n]))
        copies[n].start()
    for copy in copies:
        copy.wait()


def call(kernel, shapes, args, scratch=(), flops=0, vmem=32, whole=(), out_space=pltpu.VMEM, aliases={}):
    specs = []
    for n in range(len(args)):
        space = pl.ANY if n in whole else pltpu.VMEM
        specs.append(pl.BlockSpec(memory_space=space))
    return pl.pallas_call(
        kernel,
        out_shape=[jax.ShapeDtypeStruct(*shape) for shape in shapes],
        in_specs=specs,
        out_specs=[pl.BlockSpec(memory_space=out_space)] * len(shapes),
        input_output_aliases=aliases,
        scratch_shapes=list(scratch),
        compiler_params=pltpu.CompilerParams(vmem_limit_bytes=vmem * 1024 * 1024),
        cost_estimate=pl.CostEstimate(flops=flops, bytes_accessed=0, transcendentals=0),
    )(*args)


def on_device(
    queries, byte_keys, byte_values, w_query, w_key, w_value, w_out, d_output, patch_index, unpatch
):
    count = lax.axis_size("seq")
    onward = [(n, n + 1) for n in range(count - 1)]
    back = [(n + 1, n) for n in range(count - 1)]
    index = patch_index[None, :]
    packed = call(
        pack_kernel,
        [((2 * WINDOW + 16, 256), BF16)],
        (byte_keys, byte_values, index),
        [
            pltpu.VMEM((1, 1024), jnp.int32),
            pltpu.VMEM((2 * WINDOW + 16, 256), BF16),
            pltpu.SemaphoreType.DMA((5,)),
            pltpu.SemaphoreType.DMA((5,)),
        ],
        flops=10**6,
        vmem=60,
        whole=(0, 1, 2),
        out_space=pl.ANY,
    )[0]
    packed = lax.ppermute(packed, "seq", onward)
    grads = call(
        heads_kernel,
        [((1024, 256), BF16)],
        (d_output, w_out),
        [pltpu.VMEM((1024, 1024), BF16), pltpu.VMEM((256, 1024), BF16), pltpu.SemaphoreType.DMA((3,))],
        flops=8 * 10**9,
        vmem=58,
        whole=(0, 1),
    )[0]
    own = (grads, queries, byte_keys, byte_values)
    near, x_near = call(
        near_kernel,
        [((REACH, 512), F32), ((PATCH_DEV, 768), F32)],
        (*own, index),
        flops=8 * 10**9,
    )
    sent, k_part, v_part, q_part = call(
        far_kernel,
        [((2 * PATCH_DEV + REACH, 256), BF16), ((WINDOW, 256), BF16), ((WINDOW, 256), BF16), ((256, WINDOW), BF16)],
        (*own, packed, index, near),
        flops=8 * 10**9,
    )
    arrived = lax.ppermute(sent, "seq", back)
    x_own = call(
        last_kernel,
        [((PATCH_DEV, 768), F32)],
        (*own, index, k_part, v_part, q_part, x_near),
        flops=8 * 10**9,
    )[0]
    a, b = call(
        project_kernel,
        [((PATCH_DEV // 2, 1024), BF16)] * 2,
        (x_own, arrived, w_query, w_key, w_value),
        flops=4 * 10**8,
    )
    across = [(0, 1), (1, 0), (2, 3), (3, 2)]
    around = [(0, 3), (3, 0), (1, 2), (2, 1)]

    def pair(mine, other):
        return (mine.astype(F32) + other.astype(F32)).astype(BF16)

    a_in, b_in = lax.ppermute(a, "mp", across), lax.ppermute(b, "mp", around)
    a, b = pair(a, a_in), pair(b, b_in)
    a_in, b_in = lax.ppermute(a, "mp", around), lax.ppermute(b, "mp", across)
    half = PATCH_DEV // 2
    done = ()
    for first, mine, other in ((0, a, a_in), (half, b, b_in)):
        done = call(
            functools.partial(final_kernel, first),
            [((PATCH_DEV, 1024), BF16)],
            (mine, other, unpatch, *done),
            [pltpu.VMEM((half, 1024), BF16), pltpu.SemaphoreType.DMA((4,))],
            flops=3 * 10**8,
            whole=(3,),
            out_space=pl.ANY,
            aliases={3: 0} if done else {},
        )
    return done[0]


def solution(mesh):
    in_specs = (
        P("seq", "mp"),
        P("seq", "mp"),
        P("seq", "mp"),
        P(None, "mp"),
        P(None, "mp"),
        P(None, "mp"),
        P("mp", None),
        P("seq", None),
        P("seq"),
        P(None, "mp"),
    )
    return jax.shard_map(
        on_device, mesh=mesh, in_specs=in_specs, out_specs=P("seq", "mp"), check_vma=False
    )
```

```python
import functools

import jax
import jax.numpy as jnp
from jax import lax
from jax.experimental import pallas as pl
from jax.experimental.pallas import tpu as pltpu
from jax.sharding import PartitionSpec as P

HS = 64
WINDOW = 512
PATCH_DEV = 256
TILE = 256
REACH = 128
STRIP = 32
F32 = jnp.float32
BF16 = jnp.bfloat16


def mm(a, b):
    return lax.dot_general(a, b, (((1,), (0,)), ((), ())), preferred_element_type=F32)


def mm_t(a, b):
    return lax.dot_general(a, b, (((1,), (1,)), ((), ())), preferred_element_type=F32)


def head_parts(tile):
    head = lax.broadcasted_iota(jnp.int32, tile.shape, 1) // HS
    return [jnp.where(head == h, tile, jnp.zeros_like(tile)) for h in range(tile.shape[1] // HS)]


def one_hot(slots, first, count):
    places = lax.broadcasted_iota(jnp.int32, (count, slots.shape[1]), 0) + first
    return jnp.where(places == slots, 1.0, 0.0).astype(BF16)


def rows_of_8(x, reduce):
    return reduce(x.reshape(x.shape[0] // 8, 8, x.shape[1]), 0)


def joined(total, term, op=jnp.add):
    return term if total is None else op(total, term)


class Unit:
    def __init__(self, keys, values, keys_t, query, grad, far_bias, mid_bias, d_key, d_value, known):
        self.keys, self.values, self.keys_t = keys, values, keys_t
        self.query, self.grad = query, grad
        self.far_bias, self.mid_bias = far_bias, mid_bias
        self.known = known
        self.s, self.dp = [known.get(t, (None, None))[0] for t in range(3)], [known.get(t, (None, None))[1] for t in range(3)]
        self.d_key, self.d_value = d_key, d_value
        self.strips, self.low = {}, {}
        self.peak = self.total = self.dot = None

    def score_steps(self):
        def step(into, t, a, b):
            into[t] = mm_t(a, b)

        tiles = [t for t in (0, 2, 1) if t not in self.known]
        steps = [functools.partial(step, self.s, t, self.keys[t], self.query) for t in tiles]
        return steps + [functools.partial(step, self.dp, t, self.values[t], self.grad) for t in tiles]

    def back_steps(self):
        def step(into, t, a, b):
            into[t] = joined(into[t], mm(a[t], b))

        def query_step():
            self.d_query_t = mm(self.keys_t, jnp.concatenate(self.ds, 0))

        steps = []
        for t in range(3):
            steps.append(functools.partial(step, self.d_key, t, self.ds, self.query))
            steps.append(functools.partial(step, self.d_value, t, self.p, self.grad))
        return steps[:3] + [query_step] + steps[3:]

    def inside(self, row):
        shape = (STRIP, TILE // 2)
        ahead = lax.broadcasted_iota(jnp.int32, shape, 1) - lax.broadcasted_iota(jnp.int32, shape, 0)
        return ahead >= row % (TILE // 2)

    def edge(self, parts, row, bias=None):
        half = TILE // 2
        far, near = parts[0][row : row + STRIP], parts[2][row : row + STRIP]
        if bias is not None:
            far = far + bias
        if row < half:
            left, right = jnp.where(self.inside(row), near[:, :half], far[:, :half]), near[:, half:]
        else:
            left, right = far[:, :half], jnp.where(self.inside(row), near[:, half:], far[:, half:])
        return jnp.concatenate([left, right], 1)

    def parted(self, x, row):
        half = TILE // 2
        left, right = x[:, :half], x[:, half:]
        nil = jnp.zeros_like(left)
        ok = self.inside(row)
        if row < half:
            near, far = [jnp.where(ok, left, nil), right], [jnp.where(ok, nil, left), nil]
        else:
            near, far = [nil, jnp.where(ok, right, nil)], [left, jnp.where(ok, nil, right)]
        return jnp.concatenate(far, 1), jnp.concatenate(near, 1)

    def strip_of(self, parts, mid, row):
        return parts[1][row : row + STRIP] if mid else self.edge(parts, row)

    def soft_steps(self):
        places = [(mid, row) for mid in (False, True) for row in range(0, TILE, STRIP)]

        def peak_step(mid, row):
            if mid:
                x = self.s[1][row : row + STRIP]
                x = x if self.mid_bias is None else x + self.mid_bias
            else:
                x = self.edge(self.s, row, self.far_bias)
            self.strips[mid, row] = x
            self.peak = joined(self.peak, rows_of_8(x, jnp.max), jnp.maximum)

        def peak_end():
            self.peak = jnp.max(self.peak, axis=0, keepdims=True)

        def exp_step(mid, row):
            e = jnp.exp(self.strips[mid, row] - self.peak)
            self.strips[mid, row] = e
            self.total = joined(self.total, rows_of_8(e, jnp.sum))
            self.dot = joined(self.dot, rows_of_8(e * self.strip_of(self.dp, mid, row), jnp.sum))

        def exp_end():
            self.inverse = 1.0 / jnp.sum(self.total, axis=0, keepdims=True)
            self.row_dot = self.inverse * jnp.sum(self.dot, axis=0, keepdims=True)

        def low_step(mid, row):
            p = self.strips[mid, row] * self.inverse
            ds = p * (self.strip_of(self.dp, mid, row) - self.row_dot)
            for name, x in (("p", p), ("ds", ds)):
                if mid:
                    self.low[name, 1, row] = x.astype(BF16)
                else:
                    far, near = self.parted(x, row)
                    self.low[name, 0, row], self.low[name, 2, row] = far.astype(BF16), near.astype(BF16)

        def low_end():
            self.p, self.ds = (
                [
                    jnp.concatenate([self.low[name, t, row] for row in range(0, TILE, STRIP)], 0)
                    for t in range(3)
                ]
                for name in ("p", "ds")
            )

        steps = []
        for step, end in ((peak_step, peak_end), (exp_step, exp_end), (low_step, low_end)):
            steps += [functools.partial(step, *place) for place in places] + [end]
        return steps


def attend(tiles):
    units = []
    for query, grad, keys, values, far_bias, mid_bias, known in tiles:
        keys_t = jnp.concatenate([k.T for k in keys], 1)
        d_key, d_value = [None] * 3, [None] * 3
        q_heads = head_parts(query * jnp.asarray(HS**-0.5, BF16))
        for h, (q, g) in enumerate(zip(q_heads, head_parts(grad))):
            units.append(Unit(keys, values, keys_t[h * HS : (h + 1) * HS], q, g, far_bias, mid_bias, d_key, d_value, known(h)))
    for n in range(len(units) + 2):
        matmuls = units[n - 2].back_steps() if n >= 2 else []
        matmuls += units[n].score_steps() if n < len(units) else []
        strips = units[n - 1].soft_steps() if 1 <= n <= len(units) else []
        done = 0
        for place, step in enumerate(strips):
            step()
            while done < (place + 1) * len(matmuls) // len(strips):
                matmuls[done]()
                done += 1
        for step in matmuls[done:]:
            step()
    out = []
    heads = len(units) // len(tiles)
    for first in range(0, len(units), heads):
        own = units[first : first + heads]
        d_query_t = jnp.concatenate([unit.d_query_t for unit in own], 0) * HS**-0.5
        d_key, d_value = own[0].d_key, own[0].d_value
        out.append((d_query_t.astype(BF16), d_key, d_value))
    return out


def none_known(head):
    return {}


def tiles_of(ref, first, count=3):
    return [ref[t * TILE : (t + 1) * TILE, :] for t in range(first, first + count)]


def whole_low(parts):
    return jnp.concatenate([part.astype(BF16) for part in parts], 0)


def pack_kernel(keys, values, index_hbm, packed, index, held, sems, out_sems):
    arriving, leaving = [], []
    for n in range(4):
        source = (keys, values)[n // 2]
        first = WINDOW + n % 2 * TILE
        rows = slice(n * TILE, (n + 1) * TILE)
        arriving.append(pltpu.make_async_copy(source.at[first : first + TILE, :], held.at[rows, :], sems.at[n]))
        leaving.append(pltpu.make_async_copy(held.at[rows, :], packed.at[rows, :], out_sems.at[n]))
    places = pltpu.make_async_copy(index_hbm, index, sems.at[4])
    for copy in (places, *arriving):
        copy.start()
    places.wait()
    slots = (index[:, WINDOW:] & (PATCH_DEV - 1)).astype(F32)
    row = lax.broadcasted_iota(jnp.int32, (16, TILE), 0)
    both = jnp.where(row == 0, slots[:, :TILE], slots[:, TILE:])
    held[2 * WINDOW :, :] = both.astype(BF16)
    slots_leaving = pltpu.make_async_copy(
        held.at[2 * WINDOW :, :], packed.at[2 * WINDOW :, :], out_sems.at[4]
    )
    slots_leaving.start()
    for copy, onward in zip(arriving, leaving):
        copy.wait()
        onward.start()
    for onward in leaving:
        onward.wait()
    slots_leaving.wait()


def heads_kernel(d_output_hbm, w_out_hbm, grads, d_output, w_out, sems):
    half = d_output.shape[0] // 2
    pairs = [(w_out_hbm, w_out)]
    pairs += [(d_output_hbm.at[n : n + half, :], d_output.at[n : n + half, :]) for n in (0, half)]
    copies = [pltpu.make_async_copy(*pair, sems.at[n]) for n, pair in enumerate(pairs)]
    for copy in copies:
        copy.start()
    copies[0].wait()
    for n in range(2):
        copies[1 + n].wait()
        rows = slice(n * half, (n + 1) * half)
        grads[rows, :] = mm_t(d_output[rows, :], w_out[...]).astype(BF16)


OWN_TILES = ((0, 2, 0), (1, 1, 0), (1, 2, 1))


def held_rows(n, head):
    first = (n * 4 + head) * TILE
    return slice(first, first + TILE)


def near_kernel(grads, queries, keys, values, index, near_out, x_out, s_out, dp_out):
    rows = slice(2 * TILE, 3 * TILE)
    d_query_t, d_key, d_value = attend(
        [(queries[rows, :], grads[rows, :], tiles_of(keys, 0), tiles_of(values, 0), None, None, none_known)]
    )[0]
    slots = index[...] - lax.axis_index("seq") * PATCH_DEV
    d_key, d_value = whole_low(d_key), whole_low(d_value)
    before = one_hot(slots[:, :REACH], -REACH, REACH)
    near_out[:, :TILE] = mm(before, d_key[:REACH])
    near_out[:, TILE:] = mm(before, d_value[:REACH])
    chosen = one_hot(slots[:, : 3 * TILE], 0, PATCH_DEV)
    x_out[:, :TILE] = mm_t(chosen[:, 2 * TILE :], d_query_t)
    x_out[:, TILE : 2 * TILE] = mm(chosen, d_key)
    x_out[:, 2 * TILE :] = mm(chosen, d_value)
    scale = jnp.asarray(HS**-0.5, BF16)
    for n, (tile, _, key_tile) in enumerate(OWN_TILES):
        own, there = slice(tile * TILE, (tile + 1) * TILE), slice(key_tile * TILE, (key_tile + 1) * TILE)
        q_heads, g_heads = head_parts(queries[own, :] * scale), head_parts(grads[own, :])
        for h, (q, g) in enumerate(zip(q_heads, g_heads)):
            s_out[held_rows(n, h), :] = mm_t(keys[there, :], q)
            dp_out[held_rows(n, h), :] = mm_t(values[there, :], g)


def far_kernel(
    grads, queries, keys, values, packed, index, near, s_in, dp_in,
    sent_out, k_out, v_out, q_out,
):
    shard = lax.axis_index("seq")
    bias = jnp.where(shard > 0, 0.0, -1e30).astype(F32)
    slots = index[:, :REACH] - shard * PATCH_DEV
    all_keys = tiles_of(packed, 0, 2) + tiles_of(keys, 0, 2)
    all_values = tiles_of(packed, 2, 2) + tiles_of(values, 0, 2)
    tiles = []

    def known(tile, head):
        return {
            t: (s_in.at[held_rows(n, head), :], dp_in.at[held_rows(n, head), :])
            for n, (owner, t, _) in enumerate(OWN_TILES)
            if owner == tile
        }

    for n in range(2):
        rows = slice(n * TILE, (n + 1) * TILE)
        tiles.append(
            (
                queries[rows, :],
                grads[rows, :],
                all_keys[n : n + 3],
                all_values[n : n + 3],
                bias,
                None if n else bias,
                functools.partial(known, n),
            )
        )
    (q_first, *first), (q_second, *second) = attend(tiles)
    q_out[:, :TILE], q_out[:, TILE:] = q_first, q_second
    tail = packed[2 * WINDOW :, :].astype(F32).astype(jnp.int32)
    before = jnp.concatenate([one_hot(tail[n : n + 1], 0, PATCH_DEV) for n in range(2)], 1)
    own = one_hot(slots, -REACH, REACH)
    low = PATCH_DEV - REACH
    for n, (a, b, out) in enumerate(zip(first, second, (k_out, v_out))):
        place = n * PATCH_DEV
        gone = whole_low([a[0], a[1] + b[0]])
        out[...] = whole_low([a[2] + b[1], b[2]])
        part = mm(before, gone)
        sent_out[place : place + low, :] = part[:low].astype(BF16)
        sent_out[place + low : place + PATCH_DEV, :] = (
            part[low:] + mm(own, out[:REACH, :]) + near[:, n * TILE : (n + 1) * TILE]
        ).astype(BF16)
    sent_out[2 * PATCH_DEV :, :] = mm_t(own, q_out[:, :REACH]).astype(BF16)


def last_kernel(grads, queries, keys, values, index, k_in, v_in, q_in, x_in, x_out):
    rows = slice(3 * TILE, 4 * TILE)
    d_query_t, d_key, d_value = attend(
        [(queries[rows, :], grads[rows, :], tiles_of(keys, 1), tiles_of(values, 1), None, None, none_known)]
    )[0]
    chosen = one_hot(index[...] - lax.axis_index("seq") * PATCH_DEV, 0, PATCH_DEV)
    first, later = chosen[:, :WINDOW], chosen[:, TILE:]
    x_out[:, :TILE] = (
        x_in[:, :TILE] + mm_t(first, q_in[...]) + mm_t(chosen[:, 3 * TILE :], d_query_t)
    )
    for n, (early, parts) in enumerate(((k_in, d_key), (v_in, d_value))):
        at = slice((n + 1) * TILE, (n + 2) * TILE)
        x_out[:, at] = x_in[:, at] + mm(first, early[...]) + mm(later, whole_low(parts))


def project_kernel(x_in, arrived, w_query, w_key, w_value, first_out, second_out):
    low = PATCH_DEV - REACH
    x_query = jnp.concatenate(
        [x_in[:low, :TILE], x_in[low:, :TILE] + arrived[2 * PATCH_DEV :, :].astype(F32)], 0
    ).astype(BF16)
    x_key = (x_in[:, TILE : 2 * TILE] + arrived[:PATCH_DEV, :].astype(F32)).astype(BF16)
    x_value = (
        x_in[:, 2 * TILE :] + arrived[PATCH_DEV : 2 * PATCH_DEV, :].astype(F32)
    ).astype(BF16)
    d_up = mm_t(x_query, w_query[...]) + mm_t(x_key, w_key[...]) + mm_t(x_value, w_value[...])
    first_out[...] = d_up[: PATCH_DEV // 2].astype(BF16)
    second_out[...] = d_up[PATCH_DEV // 2 :].astype(BF16)


def final_kernel(first, mine, other, unpatch, *refs):
    out, low, sems = refs[-3:]
    total = (mine[...].astype(F32) + other[...].astype(F32)).astype(BF16)
    half = PATCH_DEV // 2
    width = low.shape[1] // sems.shape[0]
    copies = []
    for n in range(sems.shape[0]):
        at = slice(n * width, (n + 1) * width)
        low[:, at] = mm(total, unpatch[:, at]).astype(BF16)
        copies.append(pltpu.make_async_copy(low.at[:, at], out.at[first : first + half, at], sems.at[n]))
        copies[n].start()
    for copy in copies:
        copy.wait()


def call(kernel, shapes, args, scratch=(), flops=0, vmem=32, whole=(), out_space=pltpu.VMEM, aliases={}):
    specs = []
    for n in range(len(args)):
        space = pl.ANY if n in whole else pltpu.VMEM
        specs.append(pl.BlockSpec(memory_space=space))
    return pl.pallas_call(
        kernel,
        out_shape=[jax.ShapeDtypeStruct(*shape) for shape in shapes],
        in_specs=specs,
        out_specs=[pl.BlockSpec(memory_space=out_space)] * len(shapes),
        input_output_aliases=aliases,
        scratch_shapes=list(scratch),
        compiler_params=pltpu.CompilerParams(vmem_limit_bytes=vmem * 1024 * 1024),
        cost_estimate=pl.CostEstimate(flops=flops, bytes_accessed=0, transcendentals=0),
    )(*args)


def on_device(
    queries, byte_keys, byte_values, w_query, w_key, w_value, w_out, d_output, patch_index, unpatch
):
    count = lax.axis_size("seq")
    onward = [(n, n + 1) for n in range(count - 1)]
    back = [(n + 1, n) for n in range(count - 1)]
    index = patch_index[None, :]
    packed = call(
        pack_kernel,
        [((2 * WINDOW + 16, 256), BF16)],
        (byte_keys, byte_values, index),
        [
            pltpu.VMEM((1, 1024), jnp.int32),
            pltpu.VMEM((2 * WINDOW + 16, 256), BF16),
            pltpu.SemaphoreType.DMA((5,)),
            pltpu.SemaphoreType.DMA((5,)),
        ],
        flops=10**6,
        vmem=60,
        whole=(0, 1, 2),
        out_space=pl.ANY,
    )[0]
    packed = lax.ppermute(packed, "seq", onward)
    grads = call(
        heads_kernel,
        [((1024, 256), BF16)],
        (d_output, w_out),
        [pltpu.VMEM((1024, 1024), BF16), pltpu.VMEM((256, 1024), BF16), pltpu.SemaphoreType.DMA((3,))],
        flops=8 * 10**9,
        vmem=52,
        whole=(0, 1),
    )[0]
    own = (grads, queries, byte_keys, byte_values)
    near, x_near, s_own, dp_own = call(
        near_kernel,
        [((REACH, 512), F32), ((PATCH_DEV, 768), F32), ((3072, TILE), F32), ((3072, TILE), F32)],
        (*own, index),
        flops=8 * 10**9,
    )
    sent, k_part, v_part, q_part = call(
        far_kernel,
        [((2 * PATCH_DEV + REACH, 256), BF16), ((WINDOW, 256), BF16), ((WINDOW, 256), BF16), ((256, WINDOW), BF16)],
        (*own, packed, index, near, s_own, dp_own),
        flops=8 * 10**9,
    )
    arrived = lax.ppermute(sent, "seq", back)
    x_own = call(
        last_kernel,
        [((PATCH_DEV, 768), F32)],
        (*own, index, k_part, v_part, q_part, x_near),
        flops=8 * 10**9,
    )[0]
    a, b = call(
        project_kernel,
        [((PATCH_DEV // 2, 1024), BF16)] * 2,
        (x_own, arrived, w_query, w_key, w_value),
        flops=4 * 10**8,
    )
    across = [(0, 1), (1, 0), (2, 3), (3, 2)]
    around = [(0, 3), (3, 0), (1, 2), (2, 1)]

    def pair(mine, other):
        return (mine.astype(F32) + other.astype(F32)).astype(BF16)

    a_in, b_in = lax.ppermute(a, "mp", across), lax.ppermute(b, "mp", around)
    a, b = pair(a, a_in), pair(b, b_in)
    a_in, b_in = lax.ppermute(a, "mp", around), lax.ppermute(b, "mp", across)
    half = PATCH_DEV // 2
    done = ()
    for first, mine, other in ((0, a, a_in), (half, b, b_in)):
        done = call(
            functools.partial(final_kernel, first),
            [((PATCH_DEV, 1024), BF16)],
            (mine, other, unpatch, *done),
            [pltpu.VMEM((half, 1024), BF16), pltpu.SemaphoreType.DMA((4,))],
            flops=3 * 10**8,
            whole=(3,),
            out_space=pl.ANY,
            aliases={3: 0} if done else {},
        )
    return done[0]


def solution(mesh):
    in_specs = (
        P("seq", "mp"),
        P("seq", "mp"),
        P("seq", "mp"),
        P(None, "mp"),
        P(None, "mp"),
        P(None, "mp"),
        P("mp", None),
        P("seq", None),
        P("seq"),
        P(None, "mp"),
    )
    return jax.shard_map(
        on_device, mesh=mesh, in_specs=in_specs, out_specs=P("seq", "mp"), check_vma=False
    )
```

```python
import functools

import jax
import jax.numpy as jnp
from jax import lax
from jax.experimental import pallas as pl
from jax.experimental.pallas import tpu as pltpu
from jax.sharding import PartitionSpec as P

HS = 64
WINDOW = 512
PATCH_DEV = 256
TILE = 256
REACH = 128
STRIP = 32
F32 = jnp.float32
BF16 = jnp.bfloat16


def mm(a, b):
    return lax.dot_general(a, b, (((1,), (0,)), ((), ())), preferred_element_type=F32)


def mm_t(a, b):
    return lax.dot_general(a, b, (((1,), (1,)), ((), ())), preferred_element_type=F32)


def head_parts(tile):
    head = lax.broadcasted_iota(jnp.int32, tile.shape, 1) // HS
    return [jnp.where(head == h, tile, jnp.zeros_like(tile)) for h in range(tile.shape[1] // HS)]


def one_hot(slots, first, count):
    places = lax.broadcasted_iota(jnp.int32, (count, slots.shape[1]), 0) + first
    return jnp.where(places == slots, 1.0, 0.0).astype(BF16)


def rows_of_8(x, reduce):
    return reduce(x.reshape(x.shape[0] // 8, 8, x.shape[1]), 0)


def joined(total, term, op=jnp.add):
    return term if total is None else op(total, term)


class Unit:
    def __init__(self, keys, values, keys_t, query, grad, far_bias, mid_bias, d_key, d_value, known):
        self.keys, self.values, self.keys_t = keys, values, keys_t
        self.query, self.grad = query, grad
        self.far_bias, self.mid_bias = far_bias, mid_bias
        self.known = known
        self.s, self.dp = [known.get(t, (None, None))[0] for t in range(3)], [known.get(t, (None, None))[1] for t in range(3)]
        self.d_key, self.d_value = d_key, d_value
        self.strips, self.low = {}, {}
        self.peak = self.total = self.dot = None

    def score_steps(self):
        def step(into, t, a, b):
            into[t] = mm_t(a, b)

        tiles = [t for t in (0, 2, 1) if t not in self.known]
        steps = [functools.partial(step, self.s, t, self.keys[t], self.query) for t in tiles]
        return steps + [functools.partial(step, self.dp, t, self.values[t], self.grad) for t in tiles]

    def back_steps(self):
        def step(into, t, a, b):
            into[t] = joined(into[t], mm(a[t], b))

        def query_step():
            self.d_query_t = mm(self.keys_t, jnp.concatenate(self.ds, 0))

        steps = []
        for t in range(3):
            steps.append(functools.partial(step, self.d_key, t, self.ds, self.query))
            steps.append(functools.partial(step, self.d_value, t, self.p, self.grad))
        return steps[:3] + [query_step] + steps[3:]

    def inside(self, row):
        shape = (STRIP, TILE // 2)
        ahead = lax.broadcasted_iota(jnp.int32, shape, 1) - lax.broadcasted_iota(jnp.int32, shape, 0)
        return ahead >= row % (TILE // 2)

    def edge(self, parts, row, bias=None):
        half = TILE // 2
        far, near = parts[0][row : row + STRIP], parts[2][row : row + STRIP]
        if bias is not None:
            far = far + bias
        if row < half:
            left, right = jnp.where(self.inside(row), near[:, :half], far[:, :half]), near[:, half:]
        else:
            left, right = far[:, :half], jnp.where(self.inside(row), near[:, half:], far[:, half:])
        return jnp.concatenate([left, right], 1)

    def parted(self, x, row):
        half = TILE // 2
        left, right = x[:, :half], x[:, half:]
        nil = jnp.zeros_like(left)
        ok = self.inside(row)
        if row < half:
            near, far = [jnp.where(ok, left, nil), right], [jnp.where(ok, nil, left), nil]
        else:
            near, far = [nil, jnp.where(ok, right, nil)], [left, jnp.where(ok, nil, right)]
        return jnp.concatenate(far, 1), jnp.concatenate(near, 1)

    def strip_of(self, parts, mid, row):
        return parts[1][row : row + STRIP] if mid else self.edge(parts, row)

    def soft_steps(self):
        places = [(mid, row) for mid in (False, True) for row in range(0, TILE, STRIP)]

        def peak_step(mid, row):
            if mid:
                x = self.s[1][row : row + STRIP]
                x = x if self.mid_bias is None else x + self.mid_bias
            else:
                x = self.edge(self.s, row, self.far_bias)
            self.strips[mid, row] = x
            self.peak = joined(self.peak, rows_of_8(x, jnp.max), jnp.maximum)

        def peak_end():
            self.peak = jnp.max(self.peak, axis=0, keepdims=True)

        def exp_step(mid, row):
            e = jnp.exp(self.strips[mid, row] - self.peak)
            self.strips[mid, row] = e
            self.total = joined(self.total, rows_of_8(e, jnp.sum))
            self.dot = joined(self.dot, rows_of_8(e * self.strip_of(self.dp, mid, row), jnp.sum))

        def exp_end():
            self.inverse = 1.0 / jnp.sum(self.total, axis=0, keepdims=True)
            self.row_dot = self.inverse * jnp.sum(self.dot, axis=0, keepdims=True)

        def low_step(mid, row):
            p = self.strips[mid, row] * self.inverse
            ds = p * (self.strip_of(self.dp, mid, row) - self.row_dot)
            for name, x in (("p", p), ("ds", ds)):
                if mid:
                    self.low[name, 1, row] = x.astype(BF16)
                else:
                    far, near = self.parted(x, row)
                    self.low[name, 0, row], self.low[name, 2, row] = far.astype(BF16), near.astype(BF16)

        def low_end():
            self.p, self.ds = (
                [
                    jnp.concatenate([self.low[name, t, row] for row in range(0, TILE, STRIP)], 0)
                    for t in range(3)
                ]
                for name in ("p", "ds")
            )

        steps = []
        for step, end in ((peak_step, peak_end), (exp_step, exp_end), (low_step, low_end)):
            steps += [functools.partial(step, *place) for place in places] + [end]
        return steps


def attend(tiles):
    units = []
    for query, grad, keys, values, far_bias, mid_bias, known in tiles:
        keys_t = jnp.concatenate([k.T for k in keys], 1)
        d_key, d_value = [None] * 3, [None] * 3
        q_heads = head_parts(query * jnp.asarray(HS**-0.5, BF16))
        for h, (q, g) in enumerate(zip(q_heads, head_parts(grad))):
            units.append(Unit(keys, values, keys_t[h * HS : (h + 1) * HS], q, g, far_bias, mid_bias, d_key, d_value, known(h)))
    for n in range(len(units) + 2):
        matmuls = units[n - 2].back_steps() if n >= 2 else []
        matmuls += units[n].score_steps() if n < len(units) else []
        strips = units[n - 1].soft_steps() if 1 <= n <= len(units) else []
        done = 0
        for place, step in enumerate(strips):
            step()
            while done < (place + 1) * len(matmuls) // len(strips):
                matmuls[done]()
                done += 1
        for step in matmuls[done:]:
            step()
    out = []
    heads = len(units) // len(tiles)
    for first in range(0, len(units), heads):
        own = units[first : first + heads]
        d_query_t = jnp.concatenate([unit.d_query_t for unit in own], 0) * HS**-0.5
        d_key, d_value = own[0].d_key, own[0].d_value
        out.append((d_query_t.astype(BF16), d_key, d_value))
    return out


def none_known(head):
    return {}


def tiles_of(ref, first, count=3):
    return [ref[t * TILE : (t + 1) * TILE, :] for t in range(first, first + count)]


def whole_low(parts):
    return jnp.concatenate([part.astype(BF16) for part in parts], 0)


def pack_kernel(keys, values, index_hbm, packed, index, held, sems, out_sems):
    arriving, leaving = [], []
    for n in range(4):
        source = (keys, values)[n // 2]
        first = WINDOW + n % 2 * TILE
        rows = slice(n * TILE, (n + 1) * TILE)
        arriving.append(pltpu.make_async_copy(source.at[first : first + TILE, :], held.at[rows, :], sems.at[n]))
        leaving.append(pltpu.make_async_copy(held.at[rows, :], packed.at[rows, :], out_sems.at[n]))
    places = pltpu.make_async_copy(index_hbm, index, sems.at[4])
    for copy in (places, *arriving):
        copy.start()
    places.wait()
    slots = (index[:, WINDOW:] & (PATCH_DEV - 1)).astype(F32)
    row = lax.broadcasted_iota(jnp.int32, (16, TILE), 0)
    both = jnp.where(row == 0, slots[:, :TILE], slots[:, TILE:])
    held[2 * WINDOW :, :] = both.astype(BF16)
    slots_leaving = pltpu.make_async_copy(
        held.at[2 * WINDOW :, :], packed.at[2 * WINDOW :, :], out_sems.at[4]
    )
    slots_leaving.start()
    for copy, onward in zip(arriving, leaving):
        copy.wait()
        onward.start()
    for onward in leaving:
        onward.wait()
    slots_leaving.wait()


def heads_kernel(d_output_hbm, w_out_hbm, grads, d_output, w_out, sems):
    half = d_output.shape[0] // 2
    pairs = [(w_out_hbm, w_out)]
    pairs += [(d_output_hbm.at[n : n + half, :], d_output.at[n : n + half, :]) for n in (0, half)]
    copies = [pltpu.make_async_copy(*pair, sems.at[n]) for n, pair in enumerate(pairs)]
    for copy in copies:
        copy.start()
    copies[0].wait()
    for n in range(2):
        copies[1 + n].wait()
        rows = slice(n * half, (n + 1) * half)
        grads[rows, :] = mm_t(d_output[rows, :], w_out[...]).astype(BF16)


OWN_TILES = ((0, 2, 0), (1, 1, 0), (1, 2, 1))


def held_rows(n, head):
    first = (n * 4 + head) * TILE
    return slice(first, first + TILE)


def near_kernel(grads, queries, keys, values, index, near_out, x_out, s_out, dp_out):
    rows = slice(2 * TILE, 3 * TILE)
    d_query_t, d_key, d_value = attend(
        [(queries[rows, :], grads[rows, :], tiles_of(keys, 0), tiles_of(values, 0), None, None, none_known)]
    )[0]
    slots = index[...] - lax.axis_index("seq") * PATCH_DEV
    d_key, d_value = whole_low(d_key), whole_low(d_value)
    before = one_hot(slots[:, :REACH], -REACH, REACH)
    near_out[:, :TILE] = mm(before, d_key[:REACH])
    near_out[:, TILE:] = mm(before, d_value[:REACH])
    chosen = one_hot(slots[:, : 3 * TILE], 0, PATCH_DEV)
    x_out[:, :TILE] = mm_t(chosen[:, 2 * TILE :], d_query_t)
    x_out[:, TILE : 2 * TILE] = mm(chosen, d_key)
    x_out[:, 2 * TILE :] = mm(chosen, d_value)
    scale = jnp.asarray(HS**-0.5, BF16)
    for n, (tile, _, key_tile) in enumerate(OWN_TILES):
        own, there = slice(tile * TILE, (tile + 1) * TILE), slice(key_tile * TILE, (key_tile + 1) * TILE)
        q_heads, g_heads = head_parts(queries[own, :] * scale), head_parts(grads[own, :])
        for h, (q, g) in enumerate(zip(q_heads, g_heads)):
            s_out[held_rows(n, h), :] = mm_t(keys[there, :], q)
            dp_out[held_rows(n, h), :] = mm_t(values[there, :], g)


def far_kernel(
    grads, queries, keys, values, packed, index, near, s_in, dp_in,
    sent_out, k_out, v_out, q_out,
):
    shard = lax.axis_index("seq")
    bias = jnp.where(shard > 0, 0.0, -1e30).astype(F32)
    slots = index[:, :REACH] - shard * PATCH_DEV
    all_keys = tiles_of(packed, 0, 2) + tiles_of(keys, 0, 2)
    all_values = tiles_of(packed, 2, 2) + tiles_of(values, 0, 2)
    tiles = []

    def known(tile, head):
        return {
            t: (s_in.at[held_rows(n, head), :], dp_in.at[held_rows(n, head), :])
            for n, (owner, t, _) in enumerate(OWN_TILES)
            if owner == tile
        }

    for n in range(2):
        rows = slice(n * TILE, (n + 1) * TILE)
        tiles.append(
            (
                queries[rows, :],
                grads[rows, :],
                all_keys[n : n + 3],
                all_values[n : n + 3],
                bias,
                None if n else bias,
                functools.partial(known, n),
            )
        )
    (q_first, *first), (q_second, *second) = attend(tiles)
    q_out[:, :TILE], q_out[:, TILE:] = q_first, q_second
    tail = packed[2 * WINDOW :, :].astype(F32).astype(jnp.int32)
    before = jnp.concatenate([one_hot(tail[n : n + 1], 0, PATCH_DEV) for n in range(2)], 1)
    own = one_hot(slots, -REACH, REACH)
    low = PATCH_DEV - REACH
    for n, (a, b, out) in enumerate(zip(first, second, (k_out, v_out))):
        place = n * PATCH_DEV
        gone = whole_low([a[0], a[1] + b[0]])
        out[...] = whole_low([a[2] + b[1], b[2]])
        part = mm(before, gone)
        sent_out[place : place + low, :] = part[:low].astype(BF16)
        sent_out[place + low : place + PATCH_DEV, :] = (
            part[low:] + mm(own, out[:REACH, :]) + near[:, n * TILE : (n + 1) * TILE]
        ).astype(BF16)
    sent_out[2 * PATCH_DEV :, :] = mm_t(own, q_out[:, :REACH]).astype(BF16)


def last_kernel(grads, queries, keys, values, index, k_in, v_in, q_in, x_in, x_out):
    rows = slice(3 * TILE, 4 * TILE)
    d_query_t, d_key, d_value = attend(
        [(queries[rows, :], grads[rows, :], tiles_of(keys, 1), tiles_of(values, 1), None, None, none_known)]
    )[0]
    chosen = one_hot(index[...] - lax.axis_index("seq") * PATCH_DEV, 0, PATCH_DEV)
    first, later = chosen[:, :WINDOW], chosen[:, TILE:]
    x_out[:, :TILE] = (
        x_in[:, :TILE] + mm_t(first, q_in[...]) + mm_t(chosen[:, 3 * TILE :], d_query_t)
    )
    for n, (early, parts) in enumerate(((k_in, d_key), (v_in, d_value))):
        at = slice((n + 1) * TILE, (n + 2) * TILE)
        x_out[:, at] = x_in[:, at] + mm(first, early[...]) + mm(later, whole_low(parts))


def project_kernel(x_in, arrived, w_query, w_key, w_value, first_out, second_out):
    low = PATCH_DEV - REACH
    x_query = jnp.concatenate(
        [x_in[:low, :TILE], x_in[low:, :TILE] + arrived[2 * PATCH_DEV :, :].astype(F32)], 0
    ).astype(BF16)
    x_key = (x_in[:, TILE : 2 * TILE] + arrived[:PATCH_DEV, :].astype(F32)).astype(BF16)
    x_value = (
        x_in[:, 2 * TILE :] + arrived[PATCH_DEV : 2 * PATCH_DEV, :].astype(F32)
    ).astype(BF16)
    d_up = mm_t(x_query, w_query[...]) + mm_t(x_key, w_key[...]) + mm_t(x_value, w_value[...])
    first_out[...] = d_up[: PATCH_DEV // 2].astype(BF16)
    second_out[...] = d_up[PATCH_DEV // 2 :].astype(BF16)


def final_kernel(first, mine, other, unpatch, *refs):
    out, low, sems = refs[-3:]
    total = (mine[...].astype(F32) + other[...].astype(F32)).astype(BF16)
    half = PATCH_DEV // 2
    width = low.shape[1] // sems.shape[0]
    copies = []
    for n in range(sems.shape[0]):
        at = slice(n * width, (n + 1) * width)
        low[:, at] = mm(total, unpatch[:, at]).astype(BF16)
        copies.append(pltpu.make_async_copy(low.at[:, at], out.at[first : first + half, at], sems.at[n]))
        copies[n].start()
    for copy in copies:
        copy.wait()


def call(kernel, shapes, args, scratch=(), flops=0, vmem=32, whole=(), out_space=pltpu.VMEM, aliases={}):
    specs = []
    for n in range(len(args)):
        space = pl.ANY if n in whole else pltpu.VMEM
        specs.append(pl.BlockSpec(memory_space=space))
    return pl.pallas_call(
        kernel,
        out_shape=[jax.ShapeDtypeStruct(*shape) for shape in shapes],
        in_specs=specs,
        out_specs=[pl.BlockSpec(memory_space=out_space)] * len(shapes),
        input_output_aliases=aliases,
        scratch_shapes=list(scratch),
        compiler_params=pltpu.CompilerParams(vmem_limit_bytes=int(vmem * 1024 * 1024)),
        cost_estimate=pl.CostEstimate(flops=flops, bytes_accessed=0, transcendentals=0),
    )(*args)


def on_device(
    queries, byte_keys, byte_values, w_query, w_key, w_value, w_out, d_output, patch_index, unpatch
):
    count = lax.axis_size("seq")
    onward = [(n, n + 1) for n in range(count - 1)]
    back = [(n + 1, n) for n in range(count - 1)]
    index = patch_index[None, :]
    packed = call(
        pack_kernel,
        [((2 * WINDOW + 16, 256), BF16)],
        (byte_keys, byte_values, index),
        [
            pltpu.VMEM((1, 1024), jnp.int32),
            pltpu.VMEM((2 * WINDOW + 16, 256), BF16),
            pltpu.SemaphoreType.DMA((5,)),
            pltpu.SemaphoreType.DMA((5,)),
        ],
        flops=10**6,
        vmem=60,
        whole=(0, 1, 2),
        out_space=pl.ANY,
    )[0]
    packed = lax.ppermute(packed, "seq", onward)
    grads = call(
        heads_kernel,
        [((1024, 256), BF16)],
        (d_output, w_out),
        [pltpu.VMEM((1024, 1024), BF16), pltpu.VMEM((256, 1024), BF16), pltpu.SemaphoreType.DMA((3,))],
        flops=8 * 10**9,
        vmem=53.2,
        whole=(0, 1),
    )[0]
    own = (grads, queries, byte_keys, byte_values)
    near, x_near, s_own, dp_own = call(
        near_kernel,
        [((REACH, 512), F32), ((PATCH_DEV, 768), F32), ((3072, TILE), F32), ((3072, TILE), F32)],
        (*own, index),
        flops=8 * 10**9,
    )
    sent, k_part, v_part, q_part = call(
        far_kernel,
        [((2 * PATCH_DEV + REACH, 256), BF16), ((WINDOW, 256), BF16), ((WINDOW, 256), BF16), ((256, WINDOW), BF16)],
        (*own, packed, index, near, s_own, dp_own),
        flops=8 * 10**9,
    )
    arrived = lax.ppermute(sent, "seq", back)
    x_own = call(
        last_kernel,
        [((PATCH_DEV, 768), F32)],
        (*own, index, k_part, v_part, q_part, x_near),
        flops=8 * 10**9,
    )[0]
    a, b = call(
        project_kernel,
        [((PATCH_DEV // 2, 1024), BF16)] * 2,
        (x_own, arrived, w_query, w_key, w_value),
        flops=4 * 10**8,
    )
    across = [(0, 1), (1, 0), (2, 3), (3, 2)]
    around = [(0, 3), (3, 0), (1, 2), (2, 1)]

    def pair(mine, other):
        return (mine.astype(F32) + other.astype(F32)).astype(BF16)

    a_in, b_in = lax.ppermute(a, "mp", across), lax.ppermute(b, "mp", around)
    a, b = pair(a, a_in), pair(b, b_in)
    a_in, b_in = lax.ppermute(a, "mp", around), lax.ppermute(b, "mp", across)
    half = PATCH_DEV // 2
    done = ()
    for first, mine, other in ((0, a, a_in), (half, b, b_in)):
        done = call(
            functools.partial(final_kernel, first),
            [((PATCH_DEV, 1024), BF16)],
            (mine, other, unpatch, *done),
            [pltpu.VMEM((half, 1024), BF16), pltpu.SemaphoreType.DMA((4,))],
            flops=3 * 10**8,
            whole=(3,),
            out_space=pl.ANY,
            aliases={3: 0} if done else {},
        )
    return done[0]


def solution(mesh):
    in_specs = (
        P("seq", "mp"),
        P("seq", "mp"),
        P("seq", "mp"),
        P(None, "mp"),
        P(None, "mp"),
        P(None, "mp"),
        P("mp", None),
        P("seq", None),
        P("seq"),
        P(None, "mp"),
    )
    return jax.shard_map(
        on_device, mesh=mesh, in_specs=in_specs, out_specs=P("seq", "mp"), check_vma=False
    )
```

```python
import functools

import jax
import jax.numpy as jnp
from jax import lax
from jax.experimental import pallas as pl
from jax.experimental.pallas import tpu as pltpu
from jax.sharding import PartitionSpec as P

HS = 64
WINDOW = 512
PATCH_DEV = 256
TILE = 256
REACH = 128
STRIP = 32
F32 = jnp.float32
BF16 = jnp.bfloat16


def mm(a, b):
    return lax.dot_general(a, b, (((1,), (0,)), ((), ())), preferred_element_type=F32)


def mm_t(a, b):
    return lax.dot_general(a, b, (((1,), (1,)), ((), ())), preferred_element_type=F32)


def head_parts(tile):
    head = lax.broadcasted_iota(jnp.int32, tile.shape, 1) // HS
    return [jnp.where(head == h, tile, jnp.zeros_like(tile)) for h in range(tile.shape[1] // HS)]


def one_hot(slots, first, count):
    places = lax.broadcasted_iota(jnp.int32, (count, slots.shape[1]), 0) + first
    return jnp.where(places == slots, 1.0, 0.0).astype(BF16)


def rows_of_8(x, reduce):
    return reduce(x.reshape(x.shape[0] // 8, 8, x.shape[1]), 0)


def joined(total, term, op=jnp.add):
    return term if total is None else op(total, term)


class Unit:
    def __init__(self, keys, values, keys_t, query, grad, far_bias, mid_bias, d_key, d_value, known):
        self.keys, self.values, self.keys_t = keys, values, keys_t
        self.query, self.grad = query, grad
        self.far_bias, self.mid_bias = far_bias, mid_bias
        self.known = known
        self.s, self.dp = [known.get(t, (None, None))[0] for t in range(3)], [known.get(t, (None, None))[1] for t in range(3)]
        self.d_key, self.d_value = d_key, d_value
        self.strips, self.low = {}, {}
        self.peak = self.total = self.dot = None

    def score_steps(self):
        def step(into, t, a, b):
            into[t] = mm_t(a, b)

        tiles = [t for t in (0, 2, 1) if t not in self.known]
        steps = [functools.partial(step, self.s, t, self.keys[t], self.query) for t in tiles]
        return steps + [functools.partial(step, self.dp, t, self.values[t], self.grad) for t in tiles]

    def back_steps(self):
        def step(into, t, a, b):
            into[t] = joined(into[t], mm(a[t], b))

        def query_step():
            self.d_query_t = mm(self.keys_t, jnp.concatenate(self.ds, 0))

        steps = []
        for t in range(3):
            steps.append(functools.partial(step, self.d_key, t, self.ds, self.query))
            steps.append(functools.partial(step, self.d_value, t, self.p, self.grad))
        return steps[:3] + [query_step] + steps[3:]

    def inside(self, row):
        shape = (STRIP, TILE // 2)
        ahead = lax.broadcasted_iota(jnp.int32, shape, 1) - lax.broadcasted_iota(jnp.int32, shape, 0)
        return ahead >= row % (TILE // 2)

    def edge(self, parts, row, bias=None):
        half = TILE // 2
        far, near = parts[0][row : row + STRIP], parts[2][row : row + STRIP]
        if bias is not None:
            far = far + bias
        if row < half:
            left, right = jnp.where(self.inside(row), near[:, :half], far[:, :half]), near[:, half:]
        else:
            left, right = far[:, :half], jnp.where(self.inside(row), near[:, half:], far[:, half:])
        return jnp.concatenate([left, right], 1)

    def parted(self, x, row):
        half = TILE // 2
        left, right = x[:, :half], x[:, half:]
        nil = jnp.zeros_like(left)
        ok = self.inside(row)
        if row < half:
            near, far = [jnp.where(ok, left, nil), right], [jnp.where(ok, nil, left), nil]
        else:
            near, far = [nil, jnp.where(ok, right, nil)], [left, jnp.where(ok, nil, right)]
        return jnp.concatenate(far, 1), jnp.concatenate(near, 1)

    def strip_of(self, parts, mid, row):
        return parts[1][row : row + STRIP] if mid else self.edge(parts, row)

    def soft_steps(self):
        places = [(mid, row) for mid in (False, True) for row in range(0, TILE, STRIP)]

        def peak_step(mid, row):
            if mid:
                x = self.s[1][row : row + STRIP]
                x = x if self.mid_bias is None else x + self.mid_bias
            else:
                x = self.edge(self.s, row, self.far_bias)
            self.strips[mid, row] = x
            self.peak = joined(self.peak, rows_of_8(x, jnp.max), jnp.maximum)

        def peak_end():
            self.peak = jnp.max(self.peak, axis=0, keepdims=True)

        def exp_step(mid, row):
            e = jnp.exp(self.strips[mid, row] - self.peak)
            self.strips[mid, row] = e
            self.total = joined(self.total, rows_of_8(e, jnp.sum))
            self.dot = joined(self.dot, rows_of_8(e * self.strip_of(self.dp, mid, row), jnp.sum))

        def exp_end():
            self.inverse = 1.0 / jnp.sum(self.total, axis=0, keepdims=True)
            self.row_dot = self.inverse * jnp.sum(self.dot, axis=0, keepdims=True)

        def low_step(mid, row):
            p = self.strips[mid, row] * self.inverse
            ds = p * (self.strip_of(self.dp, mid, row) - self.row_dot)
            for name, x in (("p", p), ("ds", ds)):
                if mid:
                    self.low[name, 1, row] = x.astype(BF16)
                else:
                    far, near = self.parted(x, row)
                    self.low[name, 0, row], self.low[name, 2, row] = far.astype(BF16), near.astype(BF16)

        def low_end():
            self.p, self.ds = (
                [
                    jnp.concatenate([self.low[name, t, row] for row in range(0, TILE, STRIP)], 0)
                    for t in range(3)
                ]
                for name in ("p", "ds")
            )

        steps = []
        for step, end in ((peak_step, peak_end), (exp_step, exp_end), (low_step, low_end)):
            steps += [functools.partial(step, *place) for place in places] + [end]
        return steps


def attend(tiles):
    units = []
    for query, grad, keys, values, far_bias, mid_bias, known in tiles:
        keys_t = jnp.concatenate([k.T for k in keys], 1)
        d_key, d_value = [None] * 3, [None] * 3
        q_heads = head_parts(query * jnp.asarray(HS**-0.5, BF16))
        for h, (q, g) in enumerate(zip(q_heads, head_parts(grad))):
            units.append(Unit(keys, values, keys_t[h * HS : (h + 1) * HS], q, g, far_bias, mid_bias, d_key, d_value, known(h)))
    for n in range(len(units) + 2):
        matmuls = units[n - 2].back_steps() if n >= 2 else []
        matmuls += units[n].score_steps() if n < len(units) else []
        strips = units[n - 1].soft_steps() if 1 <= n <= len(units) else []
        done = 0
        for place, step in enumerate(strips):
            step()
            while done < (place + 1) * len(matmuls) // len(strips):
                matmuls[done]()
                done += 1
        for step in matmuls[done:]:
            step()
    out = []
    heads = len(units) // len(tiles)
    for first in range(0, len(units), heads):
        own = units[first : first + heads]
        d_query_t = jnp.concatenate([unit.d_query_t for unit in own], 0) * HS**-0.5
        d_key, d_value = own[0].d_key, own[0].d_value
        out.append((d_query_t.astype(BF16), d_key, d_value))
    return out


def none_known(head):
    return {}


def tiles_of(ref, first, count=3):
    return [ref[t * TILE : (t + 1) * TILE, :] for t in range(first, first + count)]


def whole_low(parts):
    return jnp.concatenate([part.astype(BF16) for part in parts], 0)


def pack_kernel(keys, values, index_hbm, packed, index, held, sems, out_sems):
    arriving, leaving = [], []
    for n, source in enumerate((keys, values)):
        rows = slice(n * WINDOW, (n + 1) * WINDOW)
        arriving.append(pltpu.make_async_copy(source.at[WINDOW:, :], held.at[rows, :], sems.at[n]))
        leaving.append(pltpu.make_async_copy(held.at[rows, :], packed.at[rows, :], out_sems.at[n]))
    places = pltpu.make_async_copy(index_hbm, index, sems.at[2])
    for copy in (places, *arriving):
        copy.start()
    places.wait()
    slots = (index[:, WINDOW:] & (PATCH_DEV - 1)).astype(F32)
    row = lax.broadcasted_iota(jnp.int32, (16, TILE), 0)
    both = jnp.where(row == 0, slots[:, :TILE], slots[:, TILE:])
    held[2 * WINDOW :, :] = both.astype(BF16)
    slots_leaving = pltpu.make_async_copy(
        held.at[2 * WINDOW :, :], packed.at[2 * WINDOW :, :], out_sems.at[2]
    )
    slots_leaving.start()
    for copy, onward in zip(arriving, leaving):
        copy.wait()
        onward.start()
    for onward in leaving:
        onward.wait()
    slots_leaving.wait()


def heads_kernel(d_output_hbm, w_out_hbm, grads, d_output, w_out, sems):
    half = d_output.shape[0] // 2
    pairs = [(w_out_hbm, w_out)]
    pairs += [(d_output_hbm.at[n : n + half, :], d_output.at[n : n + half, :]) for n in (0, half)]
    copies = [pltpu.make_async_copy(*pair, sems.at[n]) for n, pair in enumerate(pairs)]
    for copy in copies:
        copy.start()
    copies[0].wait()
    for n in range(2):
        copies[1 + n].wait()
        rows = slice(n * half, (n + 1) * half)
        grads[rows, :] = mm_t(d_output[rows, :], w_out[...]).astype(BF16)


OWN_TILES = ((0, 2, 0), (1, 1, 0), (1, 2, 1))


def held_rows(n, head):
    first = (n * 4 + head) * TILE
    return slice(first, first + TILE)


def near_kernel(grads, queries, keys, values, index, near_out, x_out, s_out, dp_out):
    rows = slice(2 * TILE, 3 * TILE)
    d_query_t, d_key, d_value = attend(
        [(queries[rows, :], grads[rows, :], tiles_of(keys, 0), tiles_of(values, 0), None, None, none_known)]
    )[0]
    slots = index[...] - lax.axis_index("seq") * PATCH_DEV
    d_key, d_value = whole_low(d_key), whole_low(d_value)
    before = one_hot(slots[:, :REACH], -REACH, REACH)
    near_out[:, :TILE] = mm(before, d_key[:REACH])
    near_out[:, TILE:] = mm(before, d_value[:REACH])
    chosen = one_hot(slots[:, : 3 * TILE], 0, PATCH_DEV)
    x_out[:, :TILE] = mm_t(chosen[:, 2 * TILE :], d_query_t)
    x_out[:, TILE : 2 * TILE] = mm(chosen, d_key)
    x_out[:, 2 * TILE :] = mm(chosen, d_value)
    scale = jnp.asarray(HS**-0.5, BF16)
    for n, (tile, _, key_tile) in enumerate(OWN_TILES):
        own, there = slice(tile * TILE, (tile + 1) * TILE), slice(key_tile * TILE, (key_tile + 1) * TILE)
        q_heads, g_heads = head_parts(queries[own, :] * scale), head_parts(grads[own, :])
        for h, (q, g) in enumerate(zip(q_heads, g_heads)):
            s_out[held_rows(n, h), :] = mm_t(keys[there, :], q)
            dp_out[held_rows(n, h), :] = mm_t(values[there, :], g)


def far_kernel(
    grads, queries, keys, values, packed, index, near, s_in, dp_in,
    sent_out, k_out, v_out, q_out,
):
    shard = lax.axis_index("seq")
    bias = jnp.where(shard > 0, 0.0, -1e30).astype(F32)
    slots = index[:, :REACH] - shard * PATCH_DEV
    all_keys = tiles_of(packed, 0, 2) + tiles_of(keys, 0, 2)
    all_values = tiles_of(packed, 2, 2) + tiles_of(values, 0, 2)
    tiles = []

    def known(tile, head):
        return {
            t: (s_in.at[held_rows(n, head), :], dp_in.at[held_rows(n, head), :])
            for n, (owner, t, _) in enumerate(OWN_TILES)
            if owner == tile
        }

    for n in range(2):
        rows = slice(n * TILE, (n + 1) * TILE)
        tiles.append(
            (
                queries[rows, :],
                grads[rows, :],
                all_keys[n : n + 3],
                all_values[n : n + 3],
                bias,
                None if n else bias,
                functools.partial(known, n),
            )
        )
    (q_first, *first), (q_second, *second) = attend(tiles)
    q_out[:, :TILE], q_out[:, TILE:] = q_first, q_second
    tail = packed[2 * WINDOW :, :].astype(F32).astype(jnp.int32)
    before = jnp.concatenate([one_hot(tail[n : n + 1], 0, PATCH_DEV) for n in range(2)], 1)
    own = one_hot(slots, -REACH, REACH)
    low = PATCH_DEV - REACH
    for n, (a, b, out) in enumerate(zip(first, second, (k_out, v_out))):
        place = n * PATCH_DEV
        gone = whole_low([a[0], a[1] + b[0]])
        out[...] = whole_low([a[2] + b[1], b[2]])
        part = mm(before, gone)
        sent_out[place : place + low, :] = part[:low].astype(BF16)
        sent_out[place + low : place + PATCH_DEV, :] = (
            part[low:] + mm(own, out[:REACH, :]) + near[:, n * TILE : (n + 1) * TILE]
        ).astype(BF16)
    sent_out[2 * PATCH_DEV :, :] = mm_t(own, q_out[:, :REACH]).astype(BF16)


def last_kernel(grads, queries, keys, values, index, k_in, v_in, q_in, x_in, x_out):
    rows = slice(3 * TILE, 4 * TILE)
    d_query_t, d_key, d_value = attend(
        [(queries[rows, :], grads[rows, :], tiles_of(keys, 1), tiles_of(values, 1), None, None, none_known)]
    )[0]
    chosen = one_hot(index[...] - lax.axis_index("seq") * PATCH_DEV, 0, PATCH_DEV)
    first, later = chosen[:, :WINDOW], chosen[:, TILE:]
    x_out[:, :TILE] = (
        x_in[:, :TILE] + mm_t(first, q_in[...]) + mm_t(chosen[:, 3 * TILE :], d_query_t)
    )
    for n, (early, parts) in enumerate(((k_in, d_key), (v_in, d_value))):
        at = slice((n + 1) * TILE, (n + 2) * TILE)
        x_out[:, at] = x_in[:, at] + mm(first, early[...]) + mm(later, whole_low(parts))


def project_kernel(x_in, arrived, w_query, w_key, w_value, first_out, second_out):
    low = PATCH_DEV - REACH
    x_query = jnp.concatenate(
        [x_in[:low, :TILE], x_in[low:, :TILE] + arrived[2 * PATCH_DEV :, :].astype(F32)], 0
    ).astype(BF16)
    x_key = (x_in[:, TILE : 2 * TILE] + arrived[:PATCH_DEV, :].astype(F32)).astype(BF16)
    x_value = (
        x_in[:, 2 * TILE :] + arrived[PATCH_DEV : 2 * PATCH_DEV, :].astype(F32)
    ).astype(BF16)
    d_up = mm_t(x_query, w_query[...]) + mm_t(x_key, w_key[...]) + mm_t(x_value, w_value[...])
    first_out[...] = d_up[: PATCH_DEV // 2].astype(BF16)
    second_out[...] = d_up[PATCH_DEV // 2 :].astype(BF16)


def final_kernel(first, mine, other, unpatch, *refs):
    out, low, sems = refs[-3:]
    total = (mine[...].astype(F32) + other[...].astype(F32)).astype(BF16)
    half = PATCH_DEV // 2
    width = low.shape[1] // sems.shape[0]
    copies = []
    for n in range(sems.shape[0]):
        at = slice(n * width, (n + 1) * width)
        low[:, at] = mm(total, unpatch[:, at]).astype(BF16)
        copies.append(pltpu.make_async_copy(low.at[:, at], out.at[first : first + half, at], sems.at[n]))
        copies[n].start()
    for copy in copies:
        copy.wait()


def call(kernel, shapes, args, scratch=(), flops=0, vmem=32, whole=(), out_space=pltpu.VMEM, aliases={}):
    specs = []
    for n in range(len(args)):
        space = pl.ANY if n in whole else pltpu.VMEM
        specs.append(pl.BlockSpec(memory_space=space))
    return pl.pallas_call(
        kernel,
        out_shape=[jax.ShapeDtypeStruct(*shape) for shape in shapes],
        in_specs=specs,
        out_specs=[pl.BlockSpec(memory_space=out_space)] * len(shapes),
        input_output_aliases=aliases,
        scratch_shapes=list(scratch),
        compiler_params=pltpu.CompilerParams(vmem_limit_bytes=int(vmem * 1024 * 1024)),
        cost_estimate=pl.CostEstimate(flops=flops, bytes_accessed=0, transcendentals=0),
    )(*args)


def on_device(
    queries, byte_keys, byte_values, w_query, w_key, w_value, w_out, d_output, patch_index, unpatch
):
    count = lax.axis_size("seq")
    onward = [(n, n + 1) for n in range(count - 1)]
    back = [(n + 1, n) for n in range(count - 1)]
    index = patch_index[None, :]
    packed = call(
        pack_kernel,
        [((2 * WINDOW + 16, 256), BF16)],
        (byte_keys, byte_values, index),
        [
            pltpu.VMEM((1, 1024), jnp.int32),
            pltpu.VMEM((2 * WINDOW + 16, 256), BF16),
            pltpu.SemaphoreType.DMA((3,)),
            pltpu.SemaphoreType.DMA((3,)),
        ],
        flops=10**6,
        vmem=60,
        whole=(0, 1, 2),
        out_space=pl.ANY,
    )[0]
    packed = lax.ppermute(packed, "seq", onward)
    grads = call(
        heads_kernel,
        [((1024, 256), BF16)],
        (d_output, w_out),
        [pltpu.VMEM((1024, 1024), BF16), pltpu.VMEM((256, 1024), BF16), pltpu.SemaphoreType.DMA((3,))],
        flops=8 * 10**9,
        vmem=53.2,
        whole=(0, 1),
    )[0]
    own = (grads, queries, byte_keys, byte_values)
    near, x_near, s_own, dp_own = call(
        near_kernel,
        [((REACH, 512), F32), ((PATCH_DEV, 768), F32), ((3072, TILE), F32), ((3072, TILE), F32)],
        (*own, index),
        flops=8 * 10**9,
    )
    sent, k_part, v_part, q_part = call(
        far_kernel,
        [((2 * PATCH_DEV + REACH, 256), BF16), ((WINDOW, 256), BF16), ((WINDOW, 256), BF16), ((256, WINDOW), BF16)],
        (*own, packed, index, near, s_own, dp_own),
        flops=8 * 10**9,
    )
    arrived = lax.ppermute(sent, "seq", back)
    x_own = call(
        last_kernel,
        [((PATCH_DEV, 768), F32)],
        (*own, index, k_part, v_part, q_part, x_near),
        flops=8 * 10**9,
    )[0]
    a, b = call(
        project_kernel,
        [((PATCH_DEV // 2, 1024), BF16)] * 2,
        (x_own, arrived, w_query, w_key, w_value),
        flops=4 * 10**8,
    )
    across = [(0, 1), (1, 0), (2, 3), (3, 2)]
    around = [(0, 3), (3, 0), (1, 2), (2, 1)]

    def pair(mine, other):
        return (mine.astype(F32) + other.astype(F32)).astype(BF16)

    a_in, b_in = lax.ppermute(a, "mp", across), lax.ppermute(b, "mp", around)
    a, b = pair(a, a_in), pair(b, b_in)
    a_in, b_in = lax.ppermute(a, "mp", around), lax.ppermute(b, "mp", across)
    half = PATCH_DEV // 2
    done = ()
    for first, mine, other in ((0, a, a_in), (half, b, b_in)):
        done = call(
            functools.partial(final_kernel, first),
            [((PATCH_DEV, 1024), BF16)],
            (mine, other, unpatch, *done),
            [pltpu.VMEM((half, 1024), BF16), pltpu.SemaphoreType.DMA((4,))],
            flops=3 * 10**8,
            whole=(3,),
            out_space=pl.ANY,
            aliases={3: 0} if done else {},
        )
    return done[0]


def solution(mesh):
    in_specs = (
        P("seq", "mp"),
        P("seq", "mp"),
        P("seq", "mp"),
        P(None, "mp"),
        P(None, "mp"),
        P(None, "mp"),
        P("mp", None),
        P("seq", None),
        P("seq"),
        P(None, "mp"),
    )
    return jax.shard_map(
        on_device, mesh=mesh, in_specs=in_specs, out_specs=P("seq", "mp"), check_vma=False
    )
```
